512 devices in a mesh: seq: 64 (over z_hi, y, x), head: 8 (over z_lo, core).
Axes of the slice: x: 4, y: 8, z: 8 (z_hi: 2, z_lo: 4; z = z_hi * 4 + z_lo), core: 2. Of those that a mesh axis runs over, the one named last changes fastest.
Arguments:
- query_raw: bfloat16 [64, 512, 5120], P('seq', 'head'), may hold values from -60 to 60
- key_raw: bfloat16 [64, 512, 1024], P('seq', 'head'), may hold values from -60 to 60
- value_in: bfloat16 [64, 512, 1024], P('seq', 'head'), may hold values from -6 to 6
- out_grad: bfloat16 [64, 512, 5120], P('seq', 'head'), may hold values from -6 to 6
- query_gain: float32 [5120], replicated, may hold values from 0.25 to 1.75
- key_gain: float32 [1024], replicated, may hold values from 0.25 to 1.75
- doc_blocks: int32 [96], replicated, may hold values from 1 to 4, as said below
Outputs:
- d_query: bfloat16 [64, 512, 5120], P('seq', 'head')
- d_key: bfloat16 [64, 512, 1024], P('seq', 'head')
- d_value: bfloat16 [64, 512, 1024], P('seq', 'head')
- d_query_gain: float32 [5120], replicated
- d_key_gain: float32 [1024], replicated
The draws below stay inside these ranges and needn't reach their ends.
Inputs may be any that keep to these rules, and one draw needn't show every extreme that they name: `doc_blocks`: lengths of the documents in order, in blocks of 128 tokens; they sum to 256; the first document has 1 block and the second exactly 4.
All inputs are finite; a program needn't handle non-finite values.
Results may differ from the reference program's by a relative error of at most 0.0095.
The reference program's roundings to bfloat16 on the way (of `query_norm`, `key_norm`, `probs`, `score_grads`, `query_norm_grad` and `key_norm_grad`) count: a program that leaves them out, or rounds other values in their place, can miss the bound.
Values may be sent and summed in bfloat16 or wider, within the bound.
No kernel may reach another device: no remote copies, remote signals or barrier semaphores. Data moves between devices by JAX's collectives and lax.ppermute only.
A program may use at most 64 MiB of HBM per device.

```python
import math
import jax
import jax.numpy as jnp
from jax import lax

KV_HEADS = 8
GROUP = 5
HEAD_DIM = 128
D = 5120
KV_WIDTH = 1024
BLOCK = 128
SEG_BLOCKS = 2
REACH = 2
SEGMENT = 256
ROWS = 512
TOKENS = 32768
DOC_MOST = 4
DOCS = 96
N_SEQ = 64


def rough_field(key, lowest, highest, width):
    normal_part = jax.random.truncated_normal(jax.random.fold_in(key, 31), -3.0, 3.0, (N_SEQ, ROWS, width), jnp.float32)
    row_scale = jnp.exp(jax.random.uniform(jax.random.fold_in(key, 32), (N_SEQ, ROWS, 1), jnp.float32, math.log(lowest), math.log(highest)))
    column_scale = jnp.exp(jax.random.uniform(jax.random.fold_in(key, 33), (width,), jnp.float32, math.log(0.3), math.log(3.0)))
    return normal_part * row_scale * column_scale


def draw_query_raw(key, part):
    key = jax.random.fold_in(key, 1)
    field = rough_field(key, 0.3, 3.0, D)
    return jnp.clip(field, -60.0, 60.0).astype(jnp.bfloat16)


def draw_key_raw(key, part):
    key = jax.random.fold_in(key, 2)
    field = rough_field(key, 0.3, 3.0, KV_WIDTH)
    return jnp.clip(field, -60.0, 60.0).astype(jnp.bfloat16)


def draw_doc_blocks(key, part):
    key = jax.random.fold_in(key, 5)
    others = DOCS - 2
    spare = 2 * N_SEQ * SEG_BLOCKS - (SEG_BLOCKS - 1) - DOC_MOST - others
    base = jax.random.randint(jax.random.fold_in(key, 1), (others,), 0, DOC_MOST).astype(jnp.int32)
    needed = spare - jnp.sum(base)
    rising = needed >= 0
    room = jnp.where(rising, DOC_MOST - 1 - base, base)
    before = jnp.cumsum(room) - room
    change = jnp.clip(jnp.abs(needed) - before, 0, room)
    lengths = 1 + base + jnp.where(rising, change, -change)
    order = jax.random.permutation(jax.random.fold_in(key, 2), others)
    lengths = lengths[order]
    head_part = jnp.array([SEG_BLOCKS - 1, DOC_MOST], jnp.int32)
    return jnp.concatenate([head_part, lengths.astype(jnp.int32)]).astype(jnp.int32)


def block_levels(own_key, shape, cuts, low, top_value):
    level = 1.0
    for position, shards_of in cuts:
        heights = jax.random.uniform(jax.random.fold_in(jax.random.fold_in(own_key, 6), position), (shards_of,), jnp.float32, low / len(cuts), top_value / len(cuts))
        level = level * jnp.repeat(jnp.exp(heights), shape[position] // shards_of).reshape((-1,) + (1,) * (len(shape) - 1 - position))
    return level


def centred(own_key, dims, deviation, reach, pieces=(), kind=jnp.bfloat16):
    level = block_levels(own_key, dims, pieces, -0.22, 0.18) if pieces else 1.0
    drawn = jax.random.normal(own_key, dims, jnp.float32) * deviation * level
    return jnp.minimum(jnp.maximum(drawn, -reach), reach).astype(kind)


def setup_inputs(seed: int = 0) -> dict:
    streams_of = jax.random.split(jax.random.key(seed), 8)
    query_raw = draw_query_raw(jax.random.fold_in(streams_of[7], 71), 0)
    key_raw = draw_key_raw(jax.random.fold_in(streams_of[7], 71), 0)
    value_in = centred(streams_of[2], (N_SEQ, ROWS, KV_WIDTH), 1.0, 6.0, ((0, 64), (1, 8)))
    out_grad = centred(streams_of[3], (N_SEQ, ROWS, D), 1.0, 6.0, ((0, 64), (1, 8)))
    query_gain = jnp.clip(1.0 + 0.15 * jax.random.normal(streams_of[4], (D,), jnp.float32), 0.25, 1.75)
    key_gain = jnp.clip(1.0 + 0.15 * jax.random.normal(streams_of[5], (KV_WIDTH,), jnp.float32), 0.25, 1.75)
    doc_blocks = draw_doc_blocks(jax.random.fold_in(streams_of[7], 71), 0)
    return {"query_raw": query_raw, "key_raw": key_raw, "value_in": value_in, "out_grad": out_grad, "query_gain": query_gain, "key_gain": key_gain, "doc_blocks": doc_blocks}


EPSILON = 1e-06
MASKED = -1e+30

def normalize(rows, gain):
    values = rows.astype(jnp.float32)
    inverse = lax.rsqrt(lax.optimization_barrier(jnp.mean(values * values, axis=-1, keepdims=True)) + EPSILON)
    return ((values * inverse * gain).astype(jnp.bfloat16), inverse)

def norm_backward(rows, inverse, gain, grad):
    values = rows.astype(jnp.float32)
    upstream = grad.astype(jnp.float32)
    scaled = upstream * gain
    inner = lax.optimization_barrier(jnp.mean(scaled * values, axis=-1, keepdims=True))
    d_rows = inverse * scaled - values * inverse * inverse * inverse * inner
    d_gain = lax.optimization_barrier(jnp.sum(upstream * values * inverse, axis=(0, 1)))
    return (d_rows.astype(jnp.bfloat16), d_gain)

def natural_order(array):
    first = array[:, :SEGMENT]
    second = array[:, SEGMENT:]
    return jnp.concatenate([first, second[::-1]], axis=0)

def stored_order(array):
    return jnp.concatenate([array[:N_SEQ], array[N_SEQ:][::-1]], axis=1)

def reference(query_raw, key_raw, value_in, out_grad, query_gain, key_gain, doc_blocks):
    query_norm, query_inverse = normalize(query_raw, query_gain)
    key_norm, key_inverse = normalize(key_raw, key_gain)
    count = 2 * N_SEQ
    query_shape = (count, SEGMENT, KV_HEADS, GROUP, HEAD_DIM)
    key_shape = (count, SEGMENT, KV_HEADS, HEAD_DIM)
    queries = natural_order(query_norm).reshape(query_shape)
    grads_out = natural_order(out_grad).reshape(query_shape)
    blank = jnp.zeros((REACH, SEGMENT, KV_HEADS, HEAD_DIM), jnp.bfloat16)
    keys = jnp.concatenate([blank, natural_order(key_norm).reshape(key_shape)], axis=0)
    values = jnp.concatenate([blank, natural_order(value_in).reshape(key_shape)], axis=0)
    ends = jnp.cumsum(doc_blocks).astype(jnp.int32)
    blocks = jnp.arange(TOKENS, dtype=jnp.int32) // BLOCK
    documents = lax.optimization_barrier(jnp.sum((ends[None, :] <= blocks[:, None]).astype(jnp.int32), axis=1)).astype(jnp.int32)
    documents = documents.reshape(count, SEGMENT)
    key_documents = jnp.concatenate([jnp.full((REACH, SEGMENT), -1, jnp.int32), documents], axis=0)
    window = (REACH + 1) * SEGMENT
    scale = 1.0 / math.sqrt(HEAD_DIM)

    def visit(carry, index):
        key_carry, value_carry = carry
        query = lax.dynamic_index_in_dim(queries, index, 0, keepdims=False).astype(jnp.float32)
        grad = lax.dynamic_index_in_dim(grads_out, index, 0, keepdims=False).astype(jnp.float32)
        key_block = lax.dynamic_slice_in_dim(keys, index, REACH + 1, 0).reshape(window, KV_HEADS, HEAD_DIM).astype(jnp.float32)
        value_block = lax.dynamic_slice_in_dim(values, index, REACH + 1, 0).reshape(window, KV_HEADS, HEAD_DIM).astype(jnp.float32)
        query_docs = lax.dynamic_index_in_dim(documents, index, 0, keepdims=False)
        key_docs = lax.dynamic_slice_in_dim(key_documents, index, REACH + 1, 0).reshape(window)
        query_places = index * SEGMENT + jnp.arange(SEGMENT, dtype=jnp.int32)
        key_places = (index - REACH) * SEGMENT + jnp.arange(window, dtype=jnp.int32)
        allowed = (query_docs[:, None] == key_docs[None, :]) & (key_places[None, :] <= query_places[:, None])
        scores = jnp.einsum('qgrd,kgd->grqk', query, key_block) * scale
        scores = jnp.where(allowed[None, None], scores, MASKED)
        highest = lax.optimization_barrier(jnp.max(scores, axis=-1, keepdims=True))
        log_total = highest + jnp.log(lax.optimization_barrier(jnp.sum(jnp.exp(scores - highest), axis=-1, keepdims=True)))
        weights = jnp.where(allowed[None, None], jnp.exp(scores - log_total), 0.0)
        probs = weights.astype(jnp.bfloat16).astype(jnp.float32)
        attended = jnp.einsum('grqk,kgd->qgrd', probs, value_block)
        delta = jnp.transpose(lax.optimization_barrier(jnp.sum(grad * attended, axis=-1)), (1, 2, 0))
        weight_grads = jnp.einsum('qgrd,kgd->grqk', grad, value_block)
        score_grads = (weights * (weight_grads - delta[..., None])).astype(jnp.bfloat16).astype(jnp.float32)
        query_grad = jnp.einsum('grqk,kgd->qgrd', score_grads, key_block) * scale
        key_part = jnp.einsum('grqk,qgrd->kgd', score_grads, query) * scale
        value_part = jnp.einsum('grqk,qgrd->kgd', probs, grad)
        key_carry = key_carry + key_part.reshape(REACH + 1, SEGMENT, KV_HEADS, HEAD_DIM)
        value_carry = value_carry + value_part.reshape(REACH + 1, SEGMENT, KV_HEADS, HEAD_DIM)
        finished = (key_carry[0], value_carry[0], query_grad.astype(jnp.bfloat16))
        key_carry = jnp.concatenate([key_carry[1:], jnp.zeros_like(key_carry[:1])], axis=0)
        value_carry = jnp.concatenate([value_carry[1:], jnp.zeros_like(value_carry[:1])], axis=0)
        return ((key_carry, value_carry), finished)
    start = jnp.zeros((REACH + 1, SEGMENT, KV_HEADS, HEAD_DIM), jnp.float32)
    final, outputs = lax.scan(visit, (start, start), jnp.arange(count, dtype=jnp.int32))
    key_grads = jnp.concatenate([outputs[0][REACH:], final[0][:REACH]], axis=0)
    value_grads = jnp.concatenate([outputs[1][REACH:], final[1][:REACH]], axis=0)
    query_norm_grad = stored_order(outputs[2].reshape(count, SEGMENT, D))
    key_norm_grad = stored_order(key_grads.astype(jnp.bfloat16).reshape(count, SEGMENT, KV_WIDTH))
    d_value = stored_order(value_grads.astype(jnp.bfloat16).reshape(count, SEGMENT, KV_WIDTH))
    d_query, d_query_gain = norm_backward(query_raw, query_inverse, query_gain, query_norm_grad)
    d_key, d_key_gain = norm_backward(key_raw, key_inverse, key_gain, key_norm_grad)
    return (d_query, d_key, d_value, d_query_gain, d_key_gain)
```

```python
import functools
import math

import jax
import jax.numpy as jnp
from jax import lax
from jax.experimental import pallas as pl
from jax.experimental.pallas import tpu as pltpu
from jax.sharding import PartitionSpec as P

GROUP = 5
HEAD_DIM = 128
BLOCK = 128
EPSILON = 1e-06
MASKED = -1e30
TEAM = 4
KV_EACH = 2
KV_COLS = KV_EACH * HEAD_DIM
Q_COLS = KV_EACH * GROUP * HEAD_DIM
SCALE = 1.0 / math.sqrt(HEAD_DIM)
LOG2E = math.log2(math.e)
F32 = jnp.float32
BF16 = jnp.bfloat16
VMEM_LIMIT = 48 * 1024 * 1024


def call(kernel, out_shape, args, smem=0, flops=0, size=0, scratch=()):
    whole = pl.BlockSpec(memory_space=pltpu.VMEM)
    scalar = pl.BlockSpec(memory_space=pltpu.SMEM)
    single = not isinstance(out_shape, (tuple, list))
    return pl.pallas_call(
        kernel,
        out_shape=out_shape,
        in_specs=[scalar] * smem + [whole] * (len(args) - smem),
        out_specs=whole if single else [whole] * len(out_shape),
        scratch_shapes=list(scratch),
        compiler_params=pltpu.CompilerParams(vmem_limit_bytes=VMEM_LIMIT),
        cost_estimate=pl.CostEstimate(flops=flops, bytes_accessed=size, transcendentals=0),
    )(*args)


def inverse_rms(values):
    return lax.rsqrt(jnp.mean(values * values, axis=-1, keepdims=True) + EPSILON)


def key_norm_kernel(key_ref, value_ref, gain_ref, out_ref):
    values = key_ref[...].astype(F32)
    normed = (values * inverse_rms(values) * gain_ref[...]).astype(BF16)
    for to in range(TEAM):
        columns = slice(to * KV_COLS, (to + 1) * KV_COLS)
        out_ref[to, :, :KV_COLS] = normed[:, columns]
        out_ref[to, :, KV_COLS:] = value_ref[:, columns]


def query_norm_kernel(segment_ref, query_ref, grad_ref, gain_ref, docs_ref, out_ref, flags_ref):
    values = query_ref[...].astype(F32)
    normed = (values * inverse_rms(values) * gain_ref[...]).astype(BF16)
    for to in range(TEAM):
        columns = slice(to * Q_COLS, (to + 1) * Q_COLS)
        out_ref[to, :, :Q_COLS] = normed[:, columns]
        out_ref[to, :, Q_COLS:] = grad_ref[:, columns]
    lengths = docs_ref[...]
    count = lengths.shape[1]
    earlier = lax.broadcasted_iota(jnp.int32, (count, count), 1) <= lax.broadcasted_iota(
        jnp.int32, (count, count), 0
    )
    ends = jnp.sum(jnp.where(earlier, lengths, 0), axis=1, keepdims=True)
    first = 2 * segment_ref[0] - 3
    places = first + lax.broadcasted_iota(jnp.int32, (count, 128), 1)
    found = jnp.sum((ends <= places).astype(jnp.int32), axis=0, keepdims=True)
    found = jnp.where(places[:1] >= 0, found, -1)
    flags_ref[...] = jnp.zeros_like(flags_ref)
    for at in range(5):
        flags_ref[at : at + 1, :] = jnp.broadcast_to(found[:, at : at + 1], (1, 128))


def contract(left, right, dims):
    return lax.dot_general(left, right, (dims, ((), ())), preferred_element_type=F32)


def attention_kernel(
    qd_ref,
    own_ref,
    near_ref,
    far_ref,
    flags_ref,
    query_gain_ref,
    key_gain_ref,
    dq_ref,
    d_own_ref,
    d_near_ref,
    d_far_ref,
    q_part_ref,
    k_part_ref,
    s_ref,
    g_ref,
    p_ref,
    ds_ref,
):
    def window(at, kind, head):
        columns = slice(kind * KV_COLS + head * HEAD_DIM, kind * KV_COLS + (head + 1) * HEAD_DIM)
        if at == 0:
            return far_ref[:, columns]
        ref = near_ref if at < 3 else own_ref
        row = (at - 1) % 2 * BLOCK
        return ref[row : row + BLOCK, columns]

    causal = lax.broadcasted_iota(jnp.int32, (BLOCK, BLOCK), 0) <= lax.broadcasted_iota(
        jnp.int32, (BLOCK, BLOCK), 1
    )
    diagonal = jnp.where(causal, 0.0, MASKED)
    factor = SCALE * LOG2E
    for head in range(KV_EACH):
        d_keys = [None] * 5
        d_values = [None] * 5
        q_part = [0.0] * GROUP
        for z in range(2):
            rows = slice(z * BLOCK, (z + 1) * BLOCK)
            blocks = list(range(z, z + 4))

            def heads_of(kind):
                base = kind * Q_COLS + head * GROUP * HEAD_DIM
                return jnp.concatenate(
                    [
                        qd_ref[rows, base + j * HEAD_DIM : base + (j + 1) * HEAD_DIM]
                        for j in range(GROUP)
                    ],
                    axis=0,
                )

            queries, grads = heads_of(0), heads_of(1)
            keys = jnp.concatenate([window(at, 0, head) for at in blocks], axis=0)
            values = jnp.concatenate([window(at, 1, head) for at in blocks], axis=0)
            s_ref[...] = contract(keys, queries, ((1,), (1,)))
            g_ref[...] = contract(values, grads, ((1,), (1,)))
            biases = []
            for place, at in enumerate(blocks):
                if place == 3:
                    biases.append(diagonal)
                else:
                    same = flags_ref[at : at + 1, :] == flags_ref[3 + z : 4 + z, :]
                    biases.append(jnp.where(same, 0.0, MASKED))
            for j in range(GROUP):
                lanes = slice(j * HEAD_DIM, (j + 1) * HEAD_DIM)
                tiles = [
                    s_ref[place * BLOCK : (place + 1) * BLOCK, lanes] * factor + biases[place]
                    for place in range(4)
                ]
                highest = functools.reduce(
                    jnp.maximum, [jnp.max(t, axis=0, keepdims=True) for t in tiles]
                )
                tiles = [jnp.exp2(t - highest) for t in tiles]
                total = functools.reduce(
                    jnp.add, [jnp.sum(t, axis=0, keepdims=True) for t in tiles]
                )
                recip = 1.0 / total
                delta = 0.0
                kept = []
                for place in range(4):
                    span = slice(place * BLOCK, (place + 1) * BLOCK)
                    weights = tiles[place] * recip
                    probs = weights.astype(BF16)
                    p_ref[span, lanes] = probs
                    kept.append(weights)
                    delta = delta + jnp.sum(
                        probs.astype(F32) * g_ref[span, lanes], axis=0, keepdims=True
                    )
                for place in range(4):
                    span = slice(place * BLOCK, (place + 1) * BLOCK)
                    ds_ref[span, lanes] = (kept[place] * (g_ref[span, lanes] - delta)).astype(BF16)
            score_grads = ds_ref[...]
            d_key = contract(score_grads, queries, ((1,), (0,)))
            d_value = contract(p_ref[...], grads, ((1,), (0,)))
            for place, at in enumerate(blocks):
                span = slice(place * BLOCK, (place + 1) * BLOCK)
                first = d_keys[at] is None
                d_keys[at] = d_key[span] if first else d_keys[at] + d_key[span]
                d_values[at] = d_value[span] if first else d_values[at] + d_value[span]
            d_query = contract(jnp.transpose(keys), score_grads, ((1,), (0,)))
            for j in range(GROUP):
                lanes = slice(j * HEAD_DIM, (j + 1) * HEAD_DIM)
                grad = (jnp.transpose(d_query[:, lanes]) * SCALE).astype(BF16)
                base = (head * GROUP + j) * HEAD_DIM
                half = BLOCK // 2
                dq_ref[2 * z, :, base : base + HEAD_DIM] = grad[:half]
                dq_ref[2 * z + 1, :, base : base + HEAD_DIM] = grad[half:]
                normed = qd_ref[rows, base : base + HEAD_DIM].astype(F32)
                q_part[j] = q_part[j] + jnp.sum(grad.astype(F32) * normed, axis=0, keepdims=True)
        for j in range(GROUP):
            base = (head * GROUP + j) * HEAD_DIM
            lanes = slice(base, base + HEAD_DIM)
            q_part_ref[:, lanes] = q_part[j] / query_gain_ref[:, lanes]
        k_part = 0.0
        key_columns = slice(head * HEAD_DIM, (head + 1) * HEAD_DIM)
        value_columns = slice(KV_COLS + head * HEAD_DIM, KV_COLS + (head + 1) * HEAD_DIM)
        for at in range(5):
            grad = d_keys[at] * SCALE
            k_part = k_part + jnp.sum(
                grad * window(at, 0, head).astype(F32), axis=0, keepdims=True
            )
            if at == 0:
                target, row = d_far_ref, 0
            else:
                target, row = (d_near_ref if at < 3 else d_own_ref), (at - 1) % 2 * BLOCK
            target[row : row + BLOCK, key_columns] = grad.astype(target.dtype)
            target[row : row + BLOCK, value_columns] = d_values[at].astype(target.dtype)
        k_part_ref[:, key_columns] = k_part / key_gain_ref[:, key_columns]


def combine_kernel(own_ref, near_ref, far_ref, out_ref):
    half = BLOCK // 2
    for to in range(TEAM):
        rows = slice(to * half, (to + 1) * half)
        total = own_ref[rows] + near_ref[rows].astype(F32)
        if to >= 2:
            total = total + far_ref[(to - 2) * half : (to - 1) * half].astype(F32)
        out_ref[to] = total.astype(BF16)


def norm_backward(rows, gain, grad):
    values = rows.astype(F32)
    inverse = inverse_rms(values)
    scaled = grad.astype(F32) * gain
    inner = jnp.mean(scaled * values, axis=-1, keepdims=True)
    return (inverse * scaled - values * (inverse * inverse * inverse * inner)).astype(BF16)


def query_back_kernel(query_ref, gain_ref, grad_ref, out_ref):
    grad = jnp.concatenate([grad_ref[at] for at in range(TEAM)], axis=1)
    out_ref[...] = norm_backward(query_ref[...], gain_ref[...], grad)


def key_back_kernel(key_ref, gain_ref, grad_ref, d_key_ref, d_value_ref):
    grad = jnp.concatenate([grad_ref[at, :, :KV_COLS] for at in range(TEAM)], axis=1)
    d_key_ref[...] = norm_backward(key_ref[...], gain_ref[...], grad)
    for at in range(TEAM):
        d_value_ref[:, at * KV_COLS : (at + 1) * KV_COLS] = grad_ref[at, :, KV_COLS:]


def shift_pairs(seq_count, steps):
    last = 2 * seq_count - 1

    def place(segment, member):
        if segment < seq_count:
            return segment * 2 * TEAM + member
        return (last - segment) * 2 * TEAM + TEAM + member

    return [
        (place(segment, member), place(segment + steps, member))
        for segment in range(2 * seq_count - steps)
        for member in range(TEAM)
    ]


def body(query_raw, key_raw, value_in, out_grad, query_gain, key_gain, doc_blocks):
    seq_count = lax.axis_size("seq")
    seq_at = lax.axis_index("seq")
    head_at = lax.axis_index("head")
    member = head_at % TEAM
    segment = jnp.where(head_at < TEAM, seq_at, 2 * seq_count - 1 - seq_at)
    teams = [list(range(TEAM)), list(range(TEAM, 2 * TEAM))]
    axes = ("seq", "head")
    rows = query_raw.shape[1]
    query_rows, key_rows, value_rows, grad_rows = (
        query_raw[0],
        key_raw[0],
        value_in[0],
        out_grad[0],
    )
    query_gain_row, key_gain_row = query_gain[None], key_gain[None]

    def exchange(array):
        return lax.all_to_all(array, "head", 0, 0, axis_index_groups=teams)

    def sent(array, steps, back=False):
        pairs = shift_pairs(seq_count, steps)
        if back:
            pairs = [(target, source) for source, target in pairs]
        return lax.ppermute(array, axes, pairs)

    kv_send = call(
        key_norm_kernel,
        jax.ShapeDtypeStruct((TEAM, rows, 2 * KV_COLS), BF16),
        (key_rows, value_rows, key_gain_row),
        size=600_000,
    )
    own = exchange(kv_send).reshape(TEAM * rows, 2 * KV_COLS)
    far = sent(own[BLOCK:], 2)
    near = sent(own, 1)
    qd_send, flags = call(
        query_norm_kernel,
        (
            jax.ShapeDtypeStruct((TEAM, rows, 2 * Q_COLS), BF16),
            jax.ShapeDtypeStruct((8, 128), jnp.int32),
        ),
        (segment[None].astype(jnp.int32), query_rows, grad_rows, query_gain_row, doc_blocks[None]),
        smem=1,
        size=3_000_000,
    )
    qd = exchange(qd_send).reshape(TEAM * rows, 2 * Q_COLS)
    my_query_gain = lax.dynamic_slice_in_dim(query_gain_row, member * Q_COLS, Q_COLS, 1)
    my_key_gain = lax.dynamic_slice_in_dim(key_gain_row, member * KV_COLS, KV_COLS, 1)
    window = 4 * BLOCK
    wide = GROUP * HEAD_DIM
    dq_send, d_own, d_near, d_far, q_part, k_part = call(
        attention_kernel,
        (
            jax.ShapeDtypeStruct((TEAM, rows, Q_COLS), BF16),
            jax.ShapeDtypeStruct((2 * BLOCK, 2 * KV_COLS), F32),
            jax.ShapeDtypeStruct((2 * BLOCK, 2 * KV_COLS), BF16),
            jax.ShapeDtypeStruct((BLOCK, 2 * KV_COLS), BF16),
            jax.ShapeDtypeStruct((1, Q_COLS), F32),
            jax.ShapeDtypeStruct((1, KV_COLS), F32),
        ),
        (qd, own, near, far, flags, my_query_gain, my_key_gain),
        flops=2 * 5 * 4 * window * wide * HEAD_DIM,
        size=5_000_000,
        scratch=[
            pltpu.VMEM((window, wide), F32),
            pltpu.VMEM((window, wide), F32),
            pltpu.VMEM((window, wide), BF16),
            pltpu.VMEM((window, wide), BF16),
        ],
    )
    back_far = sent(d_far, 2, back=True)
    back_near = sent(d_near, 1, back=True)

    part = jnp.concatenate([q_part, k_part], axis=1)
    width = part.shape[1]
    copies = lax.all_to_all(jnp.broadcast_to(part, (seq_count, width)), "seq", 0, 0, tiled=True)
    part = jnp.sum(copies, axis=0, keepdims=True)
    gains = lax.all_to_all(jnp.broadcast_to(part, (2 * TEAM, width)), "head", 0, 0, tiled=True)
    gains = gains[:TEAM] + gains[TEAM:]

    dq = exchange(dq_send)
    d_query = call(
        query_back_kernel,
        jax.ShapeDtypeStruct(query_rows.shape, BF16),
        (query_rows, query_gain_row, dq),
        size=2_000_000,
    )
    kv_back = call(
        combine_kernel,
        jax.ShapeDtypeStruct((TEAM, rows, 2 * KV_COLS), BF16),
        (d_own, back_near, back_far),
        size=1_200_000,
    )
    d_kv = exchange(kv_back)
    d_key, d_value = call(
        key_back_kernel,
        (
            jax.ShapeDtypeStruct(key_rows.shape, BF16),
            jax.ShapeDtypeStruct(value_rows.shape, BF16),
        ),
        (key_rows, key_gain_row, d_kv),
        size=700_000,
    )
    return (
        d_query[None],
        d_key[None],
        d_value[None],
        gains[:, :Q_COLS].reshape(-1),
        gains[:, Q_COLS:].reshape(-1),
    )


def solution(mesh):
    split = P("seq", "head", None)
    in_specs = (split, split, split, split, P(), P(), P())
    out_specs = (split, split, split, P(), P())
    return jax.shard_map(body, mesh=mesh, in_specs=in_specs, out_specs=out_specs, check_vma=False)
```

```python
import functools
import math

import jax
import jax.numpy as jnp
from jax import lax
from jax.experimental import pallas as pl
from jax.experimental.pallas import tpu as pltpu
from jax.sharding import PartitionSpec as P

GROUP = 5
HEAD_DIM = 128
BLOCK = 128
EPSILON = 1e-06
MASKED = -1e30
TEAM = 8
SPAN = 4
WINDOW = 2 * SPAN - 1
Q_COLS = GROUP * HEAD_DIM
KV_COLS = 2 * HEAD_DIM
BACK_COLS = Q_COLS + KV_COLS
SUM_COLS = Q_COLS + HEAD_DIM
SUM_ROWS = 16
SCALE = 1.0 / math.sqrt(HEAD_DIM)
LOG2E = math.log2(math.e)
F32 = jnp.float32
BF16 = jnp.bfloat16
VMEM_LIMIT = 32 * 1024 * 1024
VMEM_ALL = 63 * 1024 * 1024


def call(kernel, out_shape, args, smem=0, flops=0, size=1024, scratch=(), far=False):
    whole = pl.BlockSpec(memory_space=pltpu.VMEM)
    scalar = pl.BlockSpec(memory_space=pltpu.SMEM)
    given = pl.BlockSpec(memory_space=pltpu.HBM) if far else whole
    single = not isinstance(out_shape, (tuple, list))
    scratch = list(scratch)
    if far:
        arrays = args[smem:]
        scratch += [pltpu.VMEM(array.shape, array.dtype) for array in arrays]
        scratch += [pltpu.SemaphoreType.DMA((len(arrays),))]
    return pl.pallas_call(
        kernel,
        out_shape=out_shape,
        in_specs=[scalar] * smem + [given] * (len(args) - smem),
        out_specs=whole if single else [whole] * len(out_shape),
        scratch_shapes=scratch,
        compiler_params=pltpu.CompilerParams(vmem_limit_bytes=VMEM_ALL if far else VMEM_LIMIT),
        cost_estimate=pl.CostEstimate(flops=flops, bytes_accessed=size, transcendentals=0),
    )(*args)


def fetched(sources, targets, semaphores):
    copies = [
        pltpu.make_async_copy(source, target, semaphores.at[at])
        for at, (source, target) in enumerate(zip(sources, targets))
    ]
    for copy in copies:
        copy.start()
    for copy in copies:
        copy.wait()
    return targets


def inverse_rms(values):
    return lax.rsqrt(jnp.mean(values * values, axis=-1, keepdims=True) + EPSILON)


def key_norm_kernel(
    mask_ref, key_in, value_in, gain_in, out_ref, key_ref, value_ref, gain_ref, semaphores
):
    fetched((key_in, value_in, gain_in), (key_ref, value_ref, gain_ref), semaphores)
    values = key_ref[...].astype(F32)
    normed = (values * inverse_rms(values) * gain_ref[...]).astype(BF16)
    for head in range(TEAM):
        columns = slice(head * HEAD_DIM, (head + 1) * HEAD_DIM)
        slot = head ^ mask_ref[0]
        out_ref[slot, :, :HEAD_DIM] = normed[:, columns]
        out_ref[slot, :, HEAD_DIM:] = value_ref[:, columns]


def query_norm_kernel(mask_ref, span_ref, *refs):
    sources, (out_ref, flags_ref), targets, semaphores = refs[:4], refs[4:6], refs[6:10], refs[10]
    query_ref, grad_ref, gain_ref, docs_ref = fetched(sources, targets, semaphores)
    values = query_ref[...].astype(F32)
    normed = (values * inverse_rms(values) * gain_ref[...]).astype(BF16)
    for head in range(TEAM):
        columns = slice(head * Q_COLS, (head + 1) * Q_COLS)
        slot = head ^ mask_ref[0]
        out_ref[slot, :, :Q_COLS] = normed[:, columns]
        out_ref[slot, :, Q_COLS:] = grad_ref[:, columns]
    lengths = docs_ref[...]
    count = lengths.shape[1]
    earlier = lax.broadcasted_iota(jnp.int32, (count, count), 1) <= lax.broadcasted_iota(
        jnp.int32, (count, count), 0
    )
    ends = jnp.sum(jnp.where(earlier, lengths, 0), axis=1, keepdims=True)
    first = SPAN * (span_ref[0] - 1) + 1
    places = first + lax.broadcasted_iota(jnp.int32, (count, 128), 1)
    found = jnp.sum((ends <= places).astype(jnp.int32), axis=0, keepdims=True)
    found = jnp.where(places[:1] >= 0, found, -1)
    flags_ref[...] = jnp.zeros_like(flags_ref)
    for at in range(WINDOW):
        flags_ref[at : at + 1, :] = jnp.broadcast_to(found[:, at : at + 1], (1, 128))


def contract(left, right, dims):
    return lax.dot_general(left, right, (dims, ((), ())), preferred_element_type=F32)


def attention_kernel(
    qd_ref,
    own_ref,
    near_ref,
    flags_ref,
    query_gain_ref,
    key_gain_ref,
    dq_ref,
    d_own_ref,
    d_near_ref,
    part_ref,
    s_ref,
    g_ref,
    p_ref,
    ds_ref,
):
    def window(at, kind):
        columns = slice(kind * HEAD_DIM, (kind + 1) * HEAD_DIM)
        ref, row = (near_ref, at) if at < SPAN - 1 else (own_ref, at - SPAN + 1)
        return ref[row * BLOCK : (row + 1) * BLOCK, columns]

    causal = lax.broadcasted_iota(jnp.int32, (BLOCK, BLOCK), 0) <= lax.broadcasted_iota(
        jnp.int32, (BLOCK, BLOCK), 1
    )
    diagonal = jnp.where(causal, 0.0, MASKED)
    factor = SCALE * LOG2E
    half = BLOCK // 2
    copies = part_ref.shape[0]
    d_keys = [None] * WINDOW
    d_values = [None] * WINDOW
    q_part = [0.0] * GROUP
    for z in range(SPAN):
        rows = slice(z * BLOCK, (z + 1) * BLOCK)
        blocks = list(range(z, z + SPAN))

        def heads_of(kind):
            base = kind * Q_COLS
            return jnp.concatenate(
                [
                    qd_ref[rows, base + j * HEAD_DIM : base + (j + 1) * HEAD_DIM]
                    for j in range(GROUP)
                ],
                axis=0,
            )

        queries, grads = heads_of(0), heads_of(1)
        keys = jnp.concatenate([window(at, 0) for at in blocks], axis=0)
        values = jnp.concatenate([window(at, 1) for at in blocks], axis=0)
        s_ref[...] = contract(keys, queries, ((1,), (1,)))
        g_ref[...] = contract(values, grads, ((1,), (1,)))
        biases = []
        for place, at in enumerate(blocks):
            if place == SPAN - 1:
                biases.append(diagonal)
            else:
                mine = SPAN - 1 + z
                same = flags_ref[at : at + 1, :] == flags_ref[mine : mine + 1, :]
                biases.append(jnp.where(same, 0.0, MASKED))
        for j in range(GROUP):
            lanes = slice(j * HEAD_DIM, (j + 1) * HEAD_DIM)
            spans = [slice(place * BLOCK, (place + 1) * BLOCK) for place in range(SPAN)]
            tiles = [s_ref[span, lanes] * factor + bias for span, bias in zip(spans, biases)]
            highest = functools.reduce(
                jnp.maximum, [jnp.max(t, axis=0, keepdims=True) for t in tiles]
            )
            tiles = [jnp.exp2(t - highest) for t in tiles]
            total = functools.reduce(jnp.add, [jnp.sum(t, axis=0, keepdims=True) for t in tiles])
            recip = 1.0 / total
            delta = 0.0
            kept = []
            for tile, span in zip(tiles, spans):
                weights = tile * recip
                probs = weights.astype(BF16)
                p_ref[span, lanes] = probs
                kept.append(weights)
                delta = delta + jnp.sum(
                    probs.astype(F32) * g_ref[span, lanes], axis=0, keepdims=True
                )
            for weights, span in zip(kept, spans):
                ds_ref[span, lanes] = (weights * (g_ref[span, lanes] - delta)).astype(BF16)
        score_grads = ds_ref[...]
        d_key = contract(score_grads, queries, ((1,), (0,)))
        d_value = contract(p_ref[...], grads, ((1,), (0,)))
        for place, at in enumerate(blocks):
            span = slice(place * BLOCK, (place + 1) * BLOCK)
            first = d_keys[at] is None
            d_keys[at] = d_key[span] if first else d_keys[at] + d_key[span]
            d_values[at] = d_value[span] if first else d_values[at] + d_value[span]
        d_query = contract(jnp.transpose(keys), score_grads, ((1,), (0,)))
        for j in range(GROUP):
            lanes = slice(j * HEAD_DIM, (j + 1) * HEAD_DIM)
            grad = (jnp.transpose(d_query[:, lanes]) * SCALE).astype(BF16)
            dq_ref[2 * z, :, lanes] = grad[:half]
            dq_ref[2 * z + 1, :, lanes] = grad[half:]
            normed = qd_ref[rows, lanes].astype(F32)
            q_part[j] = q_part[j] + jnp.sum(grad.astype(F32) * normed, axis=0, keepdims=True)
    for j in range(GROUP):
        lanes = slice(j * HEAD_DIM, (j + 1) * HEAD_DIM)
        part_ref[:, lanes] = jnp.broadcast_to(
            q_part[j] / query_gain_ref[:, lanes], (copies, HEAD_DIM)
        )
    k_part = 0.0
    for at in range(WINDOW):
        grad = d_keys[at] * SCALE
        k_part = k_part + jnp.sum(grad * window(at, 0).astype(F32), axis=0, keepdims=True)
        target, row = (d_near_ref, at) if at < SPAN - 1 else (d_own_ref, at - SPAN + 1)
        span = slice(row * BLOCK, (row + 1) * BLOCK)
        target[span, :HEAD_DIM] = grad.astype(target.dtype)
        target[span, HEAD_DIM:] = d_values[at].astype(target.dtype)
    part_ref[:, Q_COLS:] = jnp.broadcast_to(k_part / key_gain_ref[...], (copies, HEAD_DIM))


def gather_kernel(own_ref, near_ref, dq_ref, sums_ref, out_ref):
    half = BLOCK // 2
    rest = jnp.sum(sums_ref[...], axis=0, keepdims=True)
    pieces = []
    for _ in range(3):
        pieces.append(rest.astype(BF16).astype(F32))
        rest = rest - pieces[-1]
    pieces.append(jnp.zeros((SUM_ROWS - 3, SUM_COLS), F32))
    sums = jnp.concatenate(pieces, axis=0).astype(BF16)
    for slot in range(TEAM):
        rows = slice(slot * half, (slot + 1) * half)
        total = own_ref[rows]
        if slot >= 2:
            total = total + near_ref[(slot - 2) * half : (slot - 1) * half].astype(F32)
        out_ref[slot, :half, :Q_COLS] = dq_ref[slot]
        out_ref[slot, :half, Q_COLS:] = total.astype(BF16)
        out_ref[slot, half:, :SUM_COLS] = sums
        out_ref[slot, half:, SUM_COLS:] = jnp.zeros((SUM_ROWS, BACK_COLS - SUM_COLS), BF16)


def norm_backward(rows, gain, grad):
    values = rows.astype(F32)
    inverse = inverse_rms(values)
    scaled = grad.astype(F32) * gain
    inner = jnp.mean(scaled * values, axis=-1, keepdims=True)
    return (inverse * scaled - values * (inverse * inverse * inverse * inner)).astype(BF16)


def final_kernel(
    mask_ref,
    query_ref,
    key_ref,
    query_gain_ref,
    key_gain_ref,
    back_ref,
    d_query_ref,
    d_key_ref,
    d_value_ref,
    d_query_gain_ref,
    d_key_gain_ref,
):
    half = BLOCK // 2
    slots = [head ^ mask_ref[0] for head in range(TEAM)]
    grad = jnp.concatenate([back_ref[slot, :half, :Q_COLS] for slot in slots], axis=1)
    d_query_ref[...] = norm_backward(query_ref[...], query_gain_ref[...], grad)
    keys = slice(Q_COLS, Q_COLS + HEAD_DIM)
    grad = jnp.concatenate([back_ref[slot, :half, keys] for slot in slots], axis=1)
    d_key_ref[...] = norm_backward(key_ref[...], key_gain_ref[...], grad)
    for head, slot in enumerate(slots):
        d_value_ref[:, head * HEAD_DIM : (head + 1) * HEAD_DIM] = back_ref[
            slot, :half, Q_COLS + HEAD_DIM :
        ]
        pieces = back_ref[slot, half:, :SUM_COLS].astype(F32)
        sums = pieces[0:1] + pieces[1:2] + pieces[2:3]
        d_query_gain_ref[:, head * Q_COLS : (head + 1) * Q_COLS] = sums[:, :Q_COLS]
        d_key_gain_ref[:, head * HEAD_DIM : (head + 1) * HEAD_DIM] = sums[:, Q_COLS:]


def team_of(seq_at, head_at, seq_count):
    upper = head_at // 4
    segment = seq_at + upper * (2 * seq_count - 1 - 2 * seq_at)
    slot = (segment % 2) * 4 + head_at % 4
    mask = ((seq_at // 2) % 2 ^ upper) * 4 + (seq_at // (seq_count // 2)) * 2
    return segment // 2, slot, mask


def layout(seq_count):
    spans = seq_count
    teams = [[None] * TEAM for _ in range(spans)]
    by_head = [[None] * spans for _ in range(TEAM)]
    for seq_at in range(seq_count):
        for head_at in range(TEAM):
            span, slot, mask = team_of(seq_at, head_at, seq_count)
            device = seq_at * TEAM + head_at
            teams[span][slot] = device
            by_head[slot ^ mask][span] = device
    return teams, by_head


def body(query_raw, key_raw, value_in, out_grad, query_gain, key_gain, doc_blocks):
    seq_count = lax.axis_size("seq")
    axes = ("seq", "head")
    teams, by_head = layout(seq_count)
    span, slot, mask = team_of(lax.axis_index("seq"), lax.axis_index("head"), seq_count)
    head = slot ^ mask
    mask_scalar = mask[None].astype(jnp.int32)
    span_scalar = span[None].astype(jnp.int32)
    rows = query_raw.shape[1]
    query_rows, key_rows, value_rows, grad_rows = (
        query_raw[0],
        key_raw[0],
        value_in[0],
        out_grad[0],
    )
    query_gain_row, key_gain_row = query_gain[None], key_gain[None]

    def exchange(array):
        return lax.all_to_all(array, axes, 0, 0, axis_index_groups=teams, tiled=True)

    onward = [(line[at], line[at + 1]) for line in by_head for at in range(len(line) - 1)]
    onward.sort()
    backward = sorted((target, source) for source, target in onward)

    kv_send = call(
        key_norm_kernel,
        jax.ShapeDtypeStruct((TEAM, rows, KV_COLS), BF16),
        (mask_scalar, key_rows, value_rows, key_gain_row),
        smem=1,
        far=True,
    )
    own = exchange(kv_send).reshape(TEAM * rows, KV_COLS)
    near = lax.ppermute(own[BLOCK:], axes, onward)
    qd_send, flags = call(
        query_norm_kernel,
        (
            jax.ShapeDtypeStruct((TEAM, rows, 2 * Q_COLS), BF16),
            jax.ShapeDtypeStruct((8, 128), jnp.int32),
        ),
        (mask_scalar, span_scalar, query_rows, grad_rows, query_gain_row, doc_blocks[None]),
        smem=2,
        far=True,
    )
    qd = exchange(qd_send).reshape(TEAM * rows, 2 * Q_COLS)
    my_query_gain = lax.dynamic_slice_in_dim(query_gain_row, head * Q_COLS, Q_COLS, 1)
    my_key_gain = lax.dynamic_slice_in_dim(key_gain_row, head * HEAD_DIM, HEAD_DIM, 1)
    window = SPAN * BLOCK
    dq, d_own, d_near, part = call(
        attention_kernel,
        (
            jax.ShapeDtypeStruct((TEAM, rows, Q_COLS), BF16),
            jax.ShapeDtypeStruct((window, KV_COLS), F32),
            jax.ShapeDtypeStruct((window - BLOCK, KV_COLS), BF16),
            jax.ShapeDtypeStruct((seq_count, SUM_COLS), F32),
        ),
        (qd, own, near, flags, my_query_gain, my_key_gain),
        scratch=[
            pltpu.VMEM((window, Q_COLS), F32),
            pltpu.VMEM((window, Q_COLS), F32),
            pltpu.VMEM((window, Q_COLS), BF16),
            pltpu.VMEM((window, Q_COLS), BF16),
        ],
    )
    back_near = lax.ppermute(d_near, axes, backward)

    def by_exchange(part):
        return lax.all_to_all(part, axes, 0, 0, axis_index_groups=by_head, tiled=True)

    def by_gather(part):
        return lax.all_gather(part[0], axes, axis_index_groups=by_head)

    sums = lax.cond(doc_blocks[0] >= 0, by_exchange, by_gather, part)
    back_send = call(
        gather_kernel,
        jax.ShapeDtypeStruct((TEAM, rows + SUM_ROWS, BACK_COLS), BF16),
        (d_own, back_near, dq, sums),
    )
    back = exchange(back_send)
    d_query, d_key, d_value, d_query_gain, d_key_gain = call(
        final_kernel,
        (
            jax.ShapeDtypeStruct(query_rows.shape, BF16),
            jax.ShapeDtypeStruct(key_rows.shape, BF16),
            jax.ShapeDtypeStruct(value_rows.shape, BF16),
            jax.ShapeDtypeStruct(query_gain_row.shape, F32),
            jax.ShapeDtypeStruct(key_gain_row.shape, F32),
        ),
        (mask_scalar, query_rows, key_rows, query_gain_row, key_gain_row, back),
        smem=1,
    )
    return d_query[None], d_key[None], d_value[None], d_query_gain[0], d_key_gain[0]


def solution(mesh):
    split = P("seq", "head", None)
    in_specs = (split, split, split, split, P(), P(), P())
    out_specs = (split, split, split, P(), P())
    return jax.shard_map(body, mesh=mesh, in_specs=in_specs, out_specs=out_specs, check_vma=False)
```

```python
import functools
import math

import jax
import jax.numpy as jnp
from jax import lax
from jax.experimental import pallas as pl
from jax.experimental.pallas import tpu as pltpu
from jax.sharding import PartitionSpec as P

GROUP = 5
HEAD_DIM = 128
BLOCK = 128
EPSILON = 1e-06
MASKED = -1e30
TEAM = 8
SPAN = 4
WINDOW = 2 * SPAN - 1
Q_COLS = GROUP * HEAD_DIM
KV_COLS = 2 * HEAD_DIM
TILES = GROUP + 2
SUM_ROWS = 16
SCALE = 1.0 / math.sqrt(HEAD_DIM)
LOG2E = math.log2(math.e)
F32 = jnp.float32
BF16 = jnp.bfloat16
VMEM_LIMIT = 32 * 1024 * 1024
VMEM_ALL = 63 * 1024 * 1024


def call(kernel, out_shape, args, smem=0, flops=0, size=1024, scratch=(), far=False):
    whole = pl.BlockSpec(memory_space=pltpu.VMEM)
    scalar = pl.BlockSpec(memory_space=pltpu.SMEM)
    given = pl.BlockSpec(memory_space=pltpu.HBM) if far else whole
    single = not isinstance(out_shape, (tuple, list))
    scratch = list(scratch)
    if far:
        arrays = args[smem:]
        scratch += [pltpu.VMEM(array.shape, array.dtype) for array in arrays]
        scratch += [pltpu.SemaphoreType.DMA((len(arrays),))]
    return pl.pallas_call(
        kernel,
        out_shape=out_shape,
        in_specs=[scalar] * smem + [given] * (len(args) - smem),
        out_specs=whole if single else [whole] * len(out_shape),
        scratch_shapes=scratch,
        compiler_params=pltpu.CompilerParams(vmem_limit_bytes=VMEM_ALL if far else VMEM_LIMIT),
        cost_estimate=pl.CostEstimate(flops=flops, bytes_accessed=size, transcendentals=0),
    )(*args)


def fetched(sources, targets, semaphores):
    copies = [
        pltpu.make_async_copy(source, target, semaphores.at[at])
        for at, (source, target) in enumerate(zip(sources, targets))
    ]
    for copy in copies:
        copy.start()
    for copy in copies:
        copy.wait()
    return targets


def inverse_rms(values):
    return lax.rsqrt(jnp.mean(values * values, axis=-1, keepdims=True) + EPSILON)


def key_norm_kernel(
    mask_ref, key_in, value_in, gain_in, out_ref, key_ref, value_ref, gain_ref, semaphores
):
    fetched((key_in, value_in, gain_in), (key_ref, value_ref, gain_ref), semaphores)
    values = key_ref[...].astype(F32)
    normed = (values * inverse_rms(values) * gain_ref[...]).astype(BF16)
    for head in range(TEAM):
        columns = slice(head * HEAD_DIM, (head + 1) * HEAD_DIM)
        slot = head ^ mask_ref[0]
        out_ref[slot, :, :HEAD_DIM] = normed[:, columns]
        out_ref[slot, :, HEAD_DIM:] = value_ref[:, columns]


def query_norm_kernel(mask_ref, span_ref, *refs):
    sources, (out_ref, flags_ref), targets, semaphores = refs[:4], refs[4:6], refs[6:10], refs[10]
    query_ref, grad_ref, gain_ref, docs_ref = fetched(sources, targets, semaphores)
    values = query_ref[...].astype(F32)
    normed = (values * inverse_rms(values) * gain_ref[...]).astype(BF16)
    for head in range(TEAM):
        columns = slice(head * Q_COLS, (head + 1) * Q_COLS)
        slot = head ^ mask_ref[0]
        out_ref[slot, :, :Q_COLS] = normed[:, columns]
        out_ref[slot, :, Q_COLS:] = grad_ref[:, columns]
    lengths = docs_ref[...]
    count = lengths.shape[1]
    earlier = lax.broadcasted_iota(jnp.int32, (count, count), 1) <= lax.broadcasted_iota(
        jnp.int32, (count, count), 0
    )
    ends = jnp.sum(jnp.where(earlier, lengths, 0), axis=1, keepdims=True)
    first = SPAN * (span_ref[0] - 1) + 1
    places = first + lax.broadcasted_iota(jnp.int32, (count, 128), 1)
    found = jnp.sum((ends <= places).astype(jnp.int32), axis=0, keepdims=True)
    found = jnp.where(places[:1] >= 0, found, -1)
    flags_ref[...] = jnp.zeros_like(flags_ref)
    for at in range(WINDOW):
        flags_ref[at : at + 1, :] = jnp.broadcast_to(found[:, at : at + 1], (1, 128))


def contract(left, right, dims):
    return lax.dot_general(left, right, (dims, ((), ())), preferred_element_type=F32)


def attention_kernel(
    qd_ref,
    own_ref,
    near_ref,
    flags_ref,
    dq_ref,
    d_own_ref,
    d_near_ref,
    part_ref,
    s_ref,
    g_ref,
    p_ref,
    ds_ref,
):
    def window(at, kind):
        columns = slice(kind * HEAD_DIM, (kind + 1) * HEAD_DIM)
        ref, row = (near_ref, at) if at < SPAN - 1 else (own_ref, at - SPAN + 1)
        return ref[row * BLOCK : (row + 1) * BLOCK, columns]

    causal = lax.broadcasted_iota(jnp.int32, (BLOCK, BLOCK), 0) <= lax.broadcasted_iota(
        jnp.int32, (BLOCK, BLOCK), 1
    )
    diagonal = jnp.where(causal, 0.0, MASKED)
    factor = SCALE * LOG2E
    half = BLOCK // 2
    copies = part_ref.shape[0]
    d_keys = [None] * WINDOW
    d_values = [None] * WINDOW
    q_part = [0.0] * GROUP
    for z in range(SPAN):
        rows = slice(z * BLOCK, (z + 1) * BLOCK)
        blocks = list(range(z, z + SPAN))

        def heads_of(kind):
            base = kind * Q_COLS
            return jnp.concatenate(
                [
                    qd_ref[rows, base + j * HEAD_DIM : base + (j + 1) * HEAD_DIM]
                    for j in range(GROUP)
                ],
                axis=0,
            )

        queries, grads = heads_of(0), heads_of(1)
        keys = jnp.concatenate([window(at, 0) for at in blocks], axis=0)
        values = jnp.concatenate([window(at, 1) for at in blocks], axis=0)
        s_ref[z] = contract(keys, queries, ((1,), (1,)))
        g_ref[z] = contract(values, grads, ((1,), (1,)))
        biases = []
        for place, at in enumerate(blocks):
            if place == SPAN - 1:
                biases.append(diagonal)
            else:
                mine = SPAN - 1 + z
                same = flags_ref[at : at + 1, :] == flags_ref[mine : mine + 1, :]
                biases.append(jnp.where(same, 0.0, MASKED))
        for j in range(GROUP):
            lanes = slice(j * HEAD_DIM, (j + 1) * HEAD_DIM)
            spans = [slice(place * BLOCK, (place + 1) * BLOCK) for place in range(SPAN)]
            tiles = [s_ref[z, span, lanes] * factor + bias for span, bias in zip(spans, biases)]
            highest = functools.reduce(
                jnp.maximum, [jnp.max(t, axis=0, keepdims=True) for t in tiles]
            )
            tiles = [jnp.exp2(t - highest) for t in tiles]
            total = functools.reduce(jnp.add, [jnp.sum(t, axis=0, keepdims=True) for t in tiles])
            recip = 1.0 / total
            delta = 0.0
            kept = []
            for tile, span in zip(tiles, spans):
                weights = tile * recip
                probs = weights.astype(BF16)
                p_ref[z, span, lanes] = probs
                kept.append(weights)
                delta = delta + jnp.sum(
                    probs.astype(F32) * g_ref[z, span, lanes], axis=0, keepdims=True
                )
            for weights, span in zip(kept, spans):
                ds_ref[z, span, lanes] = (weights * (g_ref[z, span, lanes] - delta)).astype(BF16)
        score_grads = ds_ref[z]
        d_key = contract(score_grads, queries, ((1,), (0,)))
        d_value = contract(p_ref[z], grads, ((1,), (0,)))
        for place, at in enumerate(blocks):
            span = slice(place * BLOCK, (place + 1) * BLOCK)
            first = d_keys[at] is None
            d_keys[at] = d_key[span] if first else d_keys[at] + d_key[span]
            d_values[at] = d_value[span] if first else d_values[at] + d_value[span]
        d_query = contract(jnp.transpose(keys), score_grads, ((1,), (0,)))
        for j in range(GROUP):
            lanes = slice(j * HEAD_DIM, (j + 1) * HEAD_DIM)
            grad = jnp.transpose(d_query[:, lanes]) * SCALE
            normed = qd_ref[rows, lanes].astype(F32)
            q_part[j] = q_part[j] + jnp.sum(grad * normed, axis=0, keepdims=True)
            grad = grad.astype(BF16)
            dq_ref[2 * z, :, lanes] = grad[:half]
            dq_ref[2 * z + 1, :, lanes] = grad[half:]
    for j in range(GROUP):
        lanes = slice(j * HEAD_DIM, (j + 1) * HEAD_DIM)
        part_ref[:, :, lanes] = jnp.broadcast_to(q_part[j][None], (copies, 1, HEAD_DIM))
    for at in range(WINDOW):
        grad = d_keys[at] * SCALE
        target, row = (d_near_ref, at) if at < SPAN - 1 else (d_own_ref, at - SPAN + 1)
        span = slice(row * BLOCK, (row + 1) * BLOCK)
        target[span, :HEAD_DIM] = grad.astype(target.dtype)
        target[span, HEAD_DIM:] = d_values[at].astype(target.dtype)


def gather_kernel(own_ref, near_ref, dq_ref, sums_ref, out_ref):
    half = BLOCK // 2
    rest = jnp.sum(sums_ref[...], axis=0)
    pieces = []
    for _ in range(3):
        piece = rest.astype(BF16).astype(F32)
        pieces += [piece[:, at : at + HEAD_DIM] for at in range(0, Q_COLS, HEAD_DIM)]
        rest = rest - piece
    pieces.append(jnp.zeros((SUM_ROWS - len(pieces), HEAD_DIM), F32))
    sums = jnp.concatenate(pieces, axis=0).astype(BF16)
    for slot in range(TEAM):
        rows = slice(slot * half, (slot + 1) * half)
        total = own_ref[rows]
        if slot >= 2:
            total = total + near_ref[(slot - 2) * half : (slot - 1) * half].astype(F32)
        total = total.astype(BF16)
        tiles = [dq_ref[slot, :, j * HEAD_DIM : (j + 1) * HEAD_DIM] for j in range(GROUP)]
        tiles += [total[:, :HEAD_DIM], total[:, HEAD_DIM:]]
        for at, tile in enumerate(tiles):
            out_ref[slot, at * half : (at + 1) * half] = tile
        out_ref[slot, TILES * half :] = sums


def norm_backward(rows, gain, grad):
    values = rows.astype(F32)
    inverse = inverse_rms(values)
    scaled = grad.astype(F32) * gain
    inner = jnp.mean(scaled * values, axis=-1, keepdims=True)
    return (inverse * scaled - values * (inverse * inverse * inverse * inner)).astype(BF16)


def final_kernel(
    mask_ref,
    query_ref,
    key_ref,
    query_gain_ref,
    key_gain_ref,
    back_ref,
    d_query_ref,
    d_key_ref,
    d_value_ref,
    d_query_gain_ref,
    d_key_gain_ref,
):
    half = BLOCK // 2
    slots = [head ^ mask_ref[0] for head in range(TEAM)]

    def tile(slot, at):
        return back_ref[slot, at * half : (at + 1) * half]

    grad = jnp.concatenate([tile(slot, at) for slot in slots for at in range(GROUP)], axis=1)
    d_query_ref[...] = norm_backward(query_ref[...], query_gain_ref[...], grad)
    grad = jnp.concatenate([tile(slot, GROUP) for slot in slots], axis=1)
    d_key_ref[...] = norm_backward(key_ref[...], key_gain_ref[...], grad)
    count = Q_COLS // HEAD_DIM
    for head, slot in enumerate(slots):
        columns = slice(head * HEAD_DIM, (head + 1) * HEAD_DIM)
        d_value_ref[:, columns] = tile(slot, GROUP + 1)
        pieces = back_ref[slot, TILES * half :].astype(F32)
        sums = pieces[:count] + pieces[count : 2 * count] + pieces[2 * count : 3 * count]
        for j in range(GROUP):
            at = slice((head * GROUP + j) * HEAD_DIM, (head * GROUP + j + 1) * HEAD_DIM)
            d_query_gain_ref[:, at] = sums[j : j + 1] / query_gain_ref[:, at]
        whole = jnp.sum(sums, axis=0, keepdims=True)
        d_key_gain_ref[:, columns] = whole / key_gain_ref[:, columns]


def team_of(seq_at, head_at, seq_count):
    upper = head_at // 4
    segment = seq_at + upper * (2 * seq_count - 1 - 2 * seq_at)
    slot = (segment % 2) * 4 + head_at % 4
    mask = ((seq_at // 2) % 2 ^ upper) * 4 + (seq_at // (seq_count // 2)) * 2
    return segment // 2, slot, mask


def layout(seq_count):
    spans = seq_count
    teams = [[None] * TEAM for _ in range(spans)]
    by_head = [[None] * spans for _ in range(TEAM)]
    for seq_at in range(seq_count):
        for head_at in range(TEAM):
            span, slot, mask = team_of(seq_at, head_at, seq_count)
            device = seq_at * TEAM + head_at
            teams[span][slot] = device
            by_head[slot ^ mask][span] = device
    return teams, by_head


def body(query_raw, key_raw, value_in, out_grad, query_gain, key_gain, doc_blocks):
    seq_count = lax.axis_size("seq")
    axes = ("seq", "head")
    teams, by_head = layout(seq_count)
    span, slot, mask = team_of(lax.axis_index("seq"), lax.axis_index("head"), seq_count)
    mask_scalar = mask[None].astype(jnp.int32)
    span_scalar = span[None].astype(jnp.int32)
    rows = query_raw.shape[1]
    query_rows, key_rows, value_rows, grad_rows = (
        query_raw[0],
        key_raw[0],
        value_in[0],
        out_grad[0],
    )
    query_gain_row, key_gain_row = query_gain[None], key_gain[None]

    def exchange(array):
        return lax.all_to_all(array, axes, 0, 0, axis_index_groups=teams, tiled=True)

    onward = [(line[at], line[at + 1]) for line in by_head for at in range(len(line) - 1)]
    onward.sort()
    backward = sorted((target, source) for source, target in onward)

    kv_send = call(
        key_norm_kernel,
        jax.ShapeDtypeStruct((TEAM, rows, KV_COLS), BF16),
        (mask_scalar, key_rows, value_rows, key_gain_row),
        smem=1,
        far=True,
    )
    own = exchange(kv_send).reshape(TEAM * rows, KV_COLS)
    near = lax.ppermute(own[BLOCK:], axes, onward)
    qd_send, flags = call(
        query_norm_kernel,
        (
            jax.ShapeDtypeStruct((TEAM, rows, 2 * Q_COLS), BF16),
            jax.ShapeDtypeStruct((8, 128), jnp.int32),
        ),
        (mask_scalar, span_scalar, query_rows, grad_rows, query_gain_row, doc_blocks[None]),
        smem=2,
        far=True,
    )
    qd = exchange(qd_send).reshape(TEAM * rows, 2 * Q_COLS)
    window = SPAN * BLOCK
    dq, d_own, d_near, part = call(
        attention_kernel,
        (
            jax.ShapeDtypeStruct((TEAM, rows, Q_COLS), BF16),
            jax.ShapeDtypeStruct((window, KV_COLS), F32),
            jax.ShapeDtypeStruct((window - BLOCK, KV_COLS), BF16),
            jax.ShapeDtypeStruct((seq_count, 1, Q_COLS), F32),
        ),
        (qd, own, near, flags),
        scratch=[
            pltpu.VMEM((SPAN, window, Q_COLS), F32),
            pltpu.VMEM((SPAN, window, Q_COLS), F32),
            pltpu.VMEM((SPAN, window, Q_COLS), BF16),
            pltpu.VMEM((SPAN, window, Q_COLS), BF16),
        ],
    )
    back_near = lax.ppermute(d_near, axes, backward)

    sums = lax.all_to_all(part, axes, 0, 0, axis_index_groups=by_head, tiled=True)
    back_send = call(
        gather_kernel,
        jax.ShapeDtypeStruct((TEAM, TILES * rows + SUM_ROWS, HEAD_DIM), BF16),
        (d_own, back_near, dq, sums),
    )
    back = exchange(back_send)
    d_query, d_key, d_value, d_query_gain, d_key_gain = call(
        final_kernel,
        (
            jax.ShapeDtypeStruct(query_rows.shape, BF16),
            jax.ShapeDtypeStruct(key_rows.shape, BF16),
            jax.ShapeDtypeStruct(value_rows.shape, BF16),
            jax.ShapeDtypeStruct(query_gain_row.shape, F32),
            jax.ShapeDtypeStruct(key_gain_row.shape, F32),
        ),
        (mask_scalar, query_rows, key_rows, query_gain_row, key_gain_row, back),
        smem=1,
    )
    return d_query[None], d_key[None], d_value[None], d_query_gain[0], d_key_gain[0]


def solution(mesh):
    split = P("seq", "head", None)
    in_specs = (split, split, split, split, P(), P(), P())
    out_specs = (split, split, split, P(), P())
    return jax.shard_map(body, mesh=mesh, in_specs=in_specs, out_specs=out_specs, check_vma=False)
```

```python
import functools
import math

import jax
import jax.numpy as jnp
from jax import lax
from jax.experimental import pallas as pl
from jax.experimental.pallas import tpu as pltpu
from jax.sharding import PartitionSpec as P

GROUP = 5
HEAD_DIM = 128
BLOCK = 128
EPSILON = 1e-06
MASKED = -1e30
TEAM = 8
SPAN = 4
WINDOW = 2 * SPAN - 1
Q_COLS = GROUP * HEAD_DIM
KV_COLS = 2 * HEAD_DIM
CHIPS = TEAM // 2
SUM_ROWS = 16
SCALE = 1.0 / math.sqrt(HEAD_DIM)
LOG2E = math.log2(math.e)
F32 = jnp.float32
BF16 = jnp.bfloat16
VMEM_LIMIT = 32 * 1024 * 1024
VMEM_ALL = 63 * 1024 * 1024


def call(kernel, out_shape, args, smem=0, flops=0, size=1024, scratch=(), far=False):
    whole = pl.BlockSpec(memory_space=pltpu.VMEM)
    scalar = pl.BlockSpec(memory_space=pltpu.SMEM)
    given = pl.BlockSpec(memory_space=pltpu.HBM) if far else whole
    single = not isinstance(out_shape, (tuple, list))
    scratch = list(scratch)
    if far:
        arrays = args[smem:]
        scratch += [pltpu.VMEM(array.shape, array.dtype) for array in arrays]
        scratch += [pltpu.SemaphoreType.DMA((len(arrays),))]
    return pl.pallas_call(
        kernel,
        out_shape=out_shape,
        in_specs=[scalar] * smem + [given] * (len(args) - smem),
        out_specs=whole if single else [whole] * len(out_shape),
        scratch_shapes=scratch,
        compiler_params=pltpu.CompilerParams(vmem_limit_bytes=VMEM_ALL if far else VMEM_LIMIT),
        cost_estimate=pl.CostEstimate(flops=flops, bytes_accessed=size, transcendentals=0),
    )(*args)


def fetched(sources, targets, semaphores):
    copies = [
        pltpu.make_async_copy(source, target, semaphores.at[at])
        for at, (source, target) in enumerate(zip(sources, targets))
    ]
    for copy in copies:
        copy.start()
    for copy in copies:
        copy.wait()
    return targets


def inverse_rms(values):
    return lax.rsqrt(jnp.mean(values * values, axis=-1, keepdims=True) + EPSILON)


def key_norm_kernel(
    mask_ref, key_in, value_in, gain_in, out_ref, key_ref, value_ref, gain_ref, semaphores
):
    fetched((key_in, value_in, gain_in), (key_ref, value_ref, gain_ref), semaphores)
    values = key_ref[...].astype(F32)
    normed = (values * inverse_rms(values) * gain_ref[...]).astype(BF16)
    for head in range(TEAM):
        columns = slice(head * HEAD_DIM, (head + 1) * HEAD_DIM)
        slot = head ^ mask_ref[0]
        out_ref[slot, :, :HEAD_DIM] = normed[:, columns]
        out_ref[slot, :, HEAD_DIM:] = value_ref[:, columns]


def query_norm_kernel(mask_ref, span_ref, *refs):
    sources, (out_ref, flags_ref), targets, semaphores = refs[:4], refs[4:6], refs[6:10], refs[10]
    query_ref, grad_ref, gain_ref, docs_ref = fetched(sources, targets, semaphores)
    values = query_ref[...].astype(F32)
    normed = (values * inverse_rms(values) * gain_ref[...]).astype(BF16)
    for head in range(TEAM):
        columns = slice(head * Q_COLS, (head + 1) * Q_COLS)
        slot = head ^ mask_ref[0]
        out_ref[slot, :, :Q_COLS] = normed[:, columns]
        out_ref[slot, :, Q_COLS:] = grad_ref[:, columns]
    lengths = docs_ref[...]
    count = lengths.shape[1]
    earlier = lax.broadcasted_iota(jnp.int32, (count, count), 1) <= lax.broadcasted_iota(
        jnp.int32, (count, count), 0
    )
    ends = jnp.sum(jnp.where(earlier, lengths, 0), axis=1, keepdims=True)
    first = SPAN * (span_ref[0] - 1) + 1
    places = first + lax.broadcasted_iota(jnp.int32, (count, 128), 1)
    found = jnp.sum((ends <= places).astype(jnp.int32), axis=0, keepdims=True)
    found = jnp.where(places[:1] >= 0, found, -1)
    flags_ref[...] = jnp.zeros_like(flags_ref)
    for at in range(WINDOW):
        flags_ref[at : at + 1, :] = jnp.broadcast_to(found[:, at : at + 1], (1, 128))


def contract(left, right, dims):
    return lax.dot_general(left, right, (dims, ((), ())), preferred_element_type=F32)


def attention_kernel(
    slot_ref,
    qd_ref,
    own_ref,
    near_ref,
    flags_ref,
    d_own_ref,
    d_near_ref,
    part_ref,
    dq_0_ref,
    dq_1_ref,
    dq_2_ref,
    dq_3_ref,
    s_ref,
    g_ref,
    p_ref,
    ds_ref,
    dq_ref,
):
    def window(at, kind):
        columns = slice(kind * HEAD_DIM, (kind + 1) * HEAD_DIM)
        ref, row = (near_ref, at) if at < SPAN - 1 else (own_ref, at - SPAN + 1)
        return ref[row * BLOCK : (row + 1) * BLOCK, columns]

    causal = lax.broadcasted_iota(jnp.int32, (BLOCK, BLOCK), 0) <= lax.broadcasted_iota(
        jnp.int32, (BLOCK, BLOCK), 1
    )
    diagonal = jnp.where(causal, 0.0, MASKED)
    factor = SCALE * LOG2E
    half = BLOCK // 2
    copies = part_ref.shape[0]
    d_keys = [None] * WINDOW
    d_values = [None] * WINDOW
    q_part = [0.0] * GROUP
    for z in range(SPAN):
        rows = slice(z * BLOCK, (z + 1) * BLOCK)
        blocks = list(range(z, z + SPAN))

        def heads_of(kind):
            base = kind * Q_COLS
            return jnp.concatenate(
                [
                    qd_ref[rows, base + j * HEAD_DIM : base + (j + 1) * HEAD_DIM]
                    for j in range(GROUP)
                ],
                axis=0,
            )

        queries, grads = heads_of(0), heads_of(1)
        keys = jnp.concatenate([window(at, 0) for at in blocks], axis=0)
        values = jnp.concatenate([window(at, 1) for at in blocks], axis=0)
        s_ref[z] = contract(keys, queries, ((1,), (1,)))
        g_ref[z] = contract(values, grads, ((1,), (1,)))
        biases = []
        for place, at in enumerate(blocks):
            if place == SPAN - 1:
                biases.append(diagonal)
            else:
                mine = SPAN - 1 + z
                same = flags_ref[at : at + 1, :] == flags_ref[mine : mine + 1, :]
                biases.append(jnp.where(same, 0.0, MASKED))
        for j in range(GROUP):
            lanes = slice(j * HEAD_DIM, (j + 1) * HEAD_DIM)
            spans = [slice(place * BLOCK, (place + 1) * BLOCK) for place in range(SPAN)]
            tiles = [s_ref[z, span, lanes] * factor + bias for span, bias in zip(spans, biases)]
            highest = functools.reduce(
                jnp.maximum, [jnp.max(t, axis=0, keepdims=True) for t in tiles]
            )
            tiles = [jnp.exp2(t - highest) for t in tiles]
            total = functools.reduce(jnp.add, [jnp.sum(t, axis=0, keepdims=True) for t in tiles])
            recip = 1.0 / total
            delta = 0.0
            kept = []
            for tile, span in zip(tiles, spans):
                weights = tile * recip
                probs = weights.astype(BF16)
                p_ref[z, span, lanes] = probs
                kept.append(weights)
                delta = delta + jnp.sum(
                    probs.astype(F32) * g_ref[z, span, lanes], axis=0, keepdims=True
                )
            for weights, span in zip(kept, spans):
                ds_ref[z, span, lanes] = (weights * (g_ref[z, span, lanes] - delta)).astype(BF16)
        score_grads = ds_ref[z]
        d_key = contract(score_grads, queries, ((1,), (0,)))
        d_value = contract(p_ref[z], grads, ((1,), (0,)))
        for place, at in enumerate(blocks):
            span = slice(place * BLOCK, (place + 1) * BLOCK)
            first = d_keys[at] is None
            d_keys[at] = d_key[span] if first else d_keys[at] + d_key[span]
            d_values[at] = d_value[span] if first else d_values[at] + d_value[span]
        d_query = contract(jnp.transpose(keys), score_grads, ((1,), (0,)))
        for j in range(GROUP):
            lanes = slice(j * HEAD_DIM, (j + 1) * HEAD_DIM)
            grad = jnp.transpose(d_query[:, lanes]) * SCALE
            normed = qd_ref[rows, lanes].astype(F32)
            q_part[j] = q_part[j] + jnp.sum(grad * normed, axis=0, keepdims=True)
            grad = grad.astype(BF16)
            dq_ref[2 * z, :, lanes] = grad[:half]
            dq_ref[2 * z + 1, :, lanes] = grad[half:]
    for j in range(GROUP):
        lanes = slice(j * HEAD_DIM, (j + 1) * HEAD_DIM)
        part_ref[:, :, lanes] = jnp.broadcast_to(q_part[j][None], (copies, 1, HEAD_DIM))
    for apart, out_ref in enumerate((dq_0_ref, dq_1_ref, dq_2_ref, dq_3_ref)):
        for core in range(2):
            out_ref[core] = dq_ref[2 * ((slot_ref[0] // 2) ^ apart) + core]
    for at in range(WINDOW):
        grad = d_keys[at] * SCALE
        target, row = (d_near_ref, at) if at < SPAN - 1 else (d_own_ref, at - SPAN + 1)
        span = slice(row * BLOCK, (row + 1) * BLOCK)
        target[span, :HEAD_DIM] = grad.astype(target.dtype)
        target[span, HEAD_DIM:] = d_values[at].astype(target.dtype)


def gather_kernel(
    slot_ref, own_ref, near_ref, sums_ref, dq_0_ref, dq_1_ref, dq_2_ref, dq_3_ref, out_ref, keep_ref, give_ref
):
    half = BLOCK // 2
    rest = jnp.sum(sums_ref[...], axis=0)
    pieces = []
    for _ in range(3):
        piece = rest.astype(BF16).astype(F32)
        pieces += [piece[:, at : at + HEAD_DIM] for at in range(0, Q_COLS, HEAD_DIM)]
        rest = rest - piece
    pieces.append(jnp.zeros((SUM_ROWS - len(pieces), HEAD_DIM), F32))
    sums = jnp.concatenate(pieces, axis=0).astype(BF16)
    for slot in range(TEAM):
        rows = slice(slot * half, (slot + 1) * half)
        total = own_ref[rows]
        if slot >= 2:
            total = total + near_ref[(slot - 2) * half : (slot - 1) * half].astype(F32)
        total = total.astype(BF16)
        out_ref[slot, :half] = total[:, :HEAD_DIM]
        out_ref[slot, half:BLOCK] = total[:, HEAD_DIM:]
        out_ref[slot, BLOCK:] = sums
    core = slot_ref[0] % 2
    for apart, dq_ref in enumerate((dq_0_ref, dq_1_ref, dq_2_ref, dq_3_ref)):
        keep_ref[apart] = dq_ref[core]
        give_ref[apart] = dq_ref[1 - core]


def norm_backward(rows, gain, grad):
    values = rows.astype(F32)
    inverse = inverse_rms(values)
    scaled = grad.astype(F32) * gain
    inner = jnp.mean(scaled * values, axis=-1, keepdims=True)
    return (inverse * scaled - values * (inverse * inverse * inverse * inner)).astype(BF16)


def query_back_kernel(head_ref, query_ref, gain_ref, kept_ref, given_ref, out_ref, grad_ref):
    for apart in range(CHIPS):
        for other, source in enumerate((kept_ref, given_ref)):
            head = head_ref[0] ^ (2 * apart + other)
            grad_ref[:, pl.ds(pl.multiple_of(head * Q_COLS, Q_COLS), Q_COLS)] = source[apart]
    out_ref[...] = norm_backward(query_ref[...], gain_ref[...], grad_ref[...])


def key_back_kernel(
    mask_ref,
    key_ref,
    query_gain_ref,
    key_gain_ref,
    back_ref,
    d_key_ref,
    d_value_ref,
    d_query_gain_ref,
    d_key_gain_ref,
):
    half = BLOCK // 2
    slots = [head ^ mask_ref[0] for head in range(TEAM)]
    grad = jnp.concatenate([back_ref[slot, :half] for slot in slots], axis=1)
    d_key_ref[...] = norm_backward(key_ref[...], key_gain_ref[...], grad)
    for head, slot in enumerate(slots):
        columns = slice(head * HEAD_DIM, (head + 1) * HEAD_DIM)
        d_value_ref[:, columns] = back_ref[slot, half:BLOCK]
        pieces = back_ref[slot, BLOCK:].astype(F32)
        sums = pieces[:GROUP] + pieces[GROUP : 2 * GROUP] + pieces[2 * GROUP : 3 * GROUP]
        for j in range(GROUP):
            at = slice((head * GROUP + j) * HEAD_DIM, (head * GROUP + j + 1) * HEAD_DIM)
            d_query_gain_ref[:, at] = sums[j : j + 1] / query_gain_ref[:, at]
        whole = jnp.sum(sums, axis=0, keepdims=True)
        d_key_gain_ref[:, columns] = whole / key_gain_ref[:, columns]


def team_of(seq_at, head_at, seq_count):
    upper = head_at // 4
    segment = seq_at + upper * (2 * seq_count - 1 - 2 * seq_at)
    slot = (segment % 2) * 4 + head_at % 4
    mask = ((seq_at // 2) % 2 ^ upper) * 4 + (seq_at // (seq_count // 2)) * 2
    return segment // 2, slot, mask


def layout(seq_count):
    spans = seq_count
    teams = [[None] * TEAM for _ in range(spans)]
    by_head = [[None] * spans for _ in range(TEAM)]
    for seq_at in range(seq_count):
        for head_at in range(TEAM):
            span, slot, mask = team_of(seq_at, head_at, seq_count)
            device = seq_at * TEAM + head_at
            teams[span][slot] = device
            by_head[slot ^ mask][span] = device
    return teams, by_head


def body(query_raw, key_raw, value_in, out_grad, query_gain, key_gain, doc_blocks):
    seq_count = lax.axis_size("seq")
    axes = ("seq", "head")
    teams, by_head = layout(seq_count)
    span, slot, mask = team_of(lax.axis_index("seq"), lax.axis_index("head"), seq_count)
    mask_scalar = mask[None].astype(jnp.int32)
    slot_scalar = slot[None].astype(jnp.int32)
    head_scalar = (slot ^ mask)[None].astype(jnp.int32)
    span_scalar = span[None].astype(jnp.int32)
    rows = query_raw.shape[1]
    query_rows, key_rows, value_rows, grad_rows = (
        query_raw[0],
        key_raw[0],
        value_in[0],
        out_grad[0],
    )
    query_gain_row, key_gain_row = query_gain[None], key_gain[None]

    def exchange(array):
        return lax.all_to_all(array, axes, 0, 0, axis_index_groups=teams, tiled=True)

    onward = [(line[at], line[at + 1]) for line in by_head for at in range(len(line) - 1)]
    onward.sort()
    backward = sorted((target, source) for source, target in onward)

    kv_send = call(
        key_norm_kernel,
        jax.ShapeDtypeStruct((TEAM, rows, KV_COLS), BF16),
        (mask_scalar, key_rows, value_rows, key_gain_row),
        smem=1,
        far=True,
    )
    own = exchange(kv_send).reshape(TEAM * rows, KV_COLS)
    near = lax.ppermute(own[BLOCK:], axes, onward)
    qd_send, flags = call(
        query_norm_kernel,
        (
            jax.ShapeDtypeStruct((TEAM, rows, 2 * Q_COLS), BF16),
            jax.ShapeDtypeStruct((8, 128), jnp.int32),
        ),
        (mask_scalar, span_scalar, query_rows, grad_rows, query_gain_row, doc_blocks[None]),
        smem=2,
        far=True,
    )
    qd = exchange(qd_send).reshape(TEAM * rows, 2 * Q_COLS)
    window = SPAN * BLOCK
    d_own, d_near, part, *dq = call(
        attention_kernel,
        (
            jax.ShapeDtypeStruct((window, KV_COLS), F32),
            jax.ShapeDtypeStruct((window - BLOCK, KV_COLS), BF16),
            jax.ShapeDtypeStruct((seq_count, 1, Q_COLS), F32),
        )
        + (jax.ShapeDtypeStruct((2, rows, Q_COLS), BF16),) * CHIPS,
        (slot_scalar, qd, own, near, flags),
        smem=1,
        scratch=[
            pltpu.VMEM((SPAN, window, Q_COLS), F32),
            pltpu.VMEM((SPAN, window, Q_COLS), F32),
            pltpu.VMEM((SPAN, window, Q_COLS), BF16),
            pltpu.VMEM((SPAN, window, Q_COLS), BF16),
            pltpu.VMEM((TEAM, rows, Q_COLS), BF16),
        ],
    )

    def within(array, apart):
        pairs = [(team[at], team[at ^ apart]) for team in teams for at in range(TEAM)]
        return lax.ppermute(array, axes, sorted(pairs))

    back_near = lax.ppermute(d_near, axes, backward)
    sums = lax.all_to_all(part, axes, 0, 0, axis_index_groups=by_head, tiled=True)
    dq = [dq[0]] + [within(dq[apart], 2 * apart) for apart in range(1, CHIPS)]
    back_send, keep, give = call(
        gather_kernel,
        (
            jax.ShapeDtypeStruct((TEAM, 2 * rows + SUM_ROWS, HEAD_DIM), BF16),
            jax.ShapeDtypeStruct((CHIPS, rows, Q_COLS), BF16),
            jax.ShapeDtypeStruct((CHIPS, rows, Q_COLS), BF16),
        ),
        (slot_scalar, d_own, back_near, sums, *dq),
        smem=1,
    )
    back = exchange(back_send)
    given = within(give, 1)
    d_query = call(
        query_back_kernel,
        jax.ShapeDtypeStruct(query_rows.shape, BF16),
        (head_scalar, query_rows, query_gain_row, keep, given),
        smem=1,
        scratch=[pltpu.VMEM(query_rows.shape, BF16)],
    )
    d_key, d_value, d_query_gain, d_key_gain = call(
        key_back_kernel,
        (
            jax.ShapeDtypeStruct(key_rows.shape, BF16),
            jax.ShapeDtypeStruct(value_rows.shape, BF16),
            jax.ShapeDtypeStruct(query_gain_row.shape, F32),
            jax.ShapeDtypeStruct(key_gain_row.shape, F32),
        ),
        (mask_scalar, key_rows, query_gain_row, key_gain_row, back),
        smem=1,
    )
    return d_query[None], d_key[None], d_value[None], d_query_gain[0], d_key_gain[0]


def solution(mesh):
    split = P("seq", "head", None)
    in_specs = (split, split, split, split, P(), P(), P())
    out_specs = (split, split, split, P(), P())
    return jax.shard_map(body, mesh=mesh, in_specs=in_specs, out_specs=out_specs, check_vma=False)
```

```python
import functools
import math

import jax
import jax.numpy as jnp
from jax import lax
from jax.experimental import pallas as pl
from jax.experimental.pallas import tpu as pltpu
from jax.sharding import PartitionSpec as P

GROUP = 5
HEAD_DIM = 128
BLOCK = 128
EPSILON = 1e-06
MASKED = -1e30
TEAM = 8
SPAN = 4
WINDOW = 2 * SPAN - 1
Q_COLS = GROUP * HEAD_DIM
KV_COLS = 2 * HEAD_DIM
CHIPS = TEAM // 2
SUM_ROWS = 16
SCALE = 1.0 / math.sqrt(HEAD_DIM)
LOG2E = math.log2(math.e)
F32 = jnp.float32
BF16 = jnp.bfloat16
VMEM_LIMIT = 14 * 1024 * 1024
VMEM_ALL = 63 * 1024 * 1024


def call(kernel, out_shape, args, smem=0, smem_out=0, flops=0, size=1024, scratch=(), far=False):
    whole = pl.BlockSpec(memory_space=pltpu.VMEM)
    scalar = pl.BlockSpec(memory_space=pltpu.SMEM)
    given = pl.BlockSpec(memory_space=pltpu.HBM) if far else whole
    single = not isinstance(out_shape, (tuple, list))
    scratch = list(scratch)
    if far:
        arrays = args[smem:]
        scratch += [pltpu.VMEM(array.shape, array.dtype) for array in arrays]
        scratch += [pltpu.SemaphoreType.DMA((len(arrays),))]
    return pl.pallas_call(
        kernel,
        out_shape=out_shape,
        in_specs=[scalar] * smem + [given] * (len(args) - smem),
        out_specs=whole
        if single
        else [whole] * (len(out_shape) - smem_out) + [scalar] * smem_out,
        scratch_shapes=scratch,
        compiler_params=pltpu.CompilerParams(vmem_limit_bytes=VMEM_ALL if far else VMEM_LIMIT),
        cost_estimate=pl.CostEstimate(flops=flops, bytes_accessed=size, transcendentals=0),
    )(*args)


def fetched(sources, targets, semaphores):
    copies = [
        pltpu.make_async_copy(source, target, semaphores.at[at])
        for at, (source, target) in enumerate(zip(sources, targets))
    ]
    for copy in copies:
        copy.start()
    for copy in copies:
        copy.wait()
    return targets


def inverse_rms(values):
    return lax.rsqrt(jnp.mean(values * values, axis=-1, keepdims=True) + EPSILON)


def key_norm_kernel(
    mask_ref, key_in, value_in, gain_in, out_ref, key_ref, value_ref, gain_ref, semaphores
):
    fetched((key_in, value_in, gain_in), (key_ref, value_ref, gain_ref), semaphores)
    values = key_ref[...].astype(F32)
    normed = (values * inverse_rms(values) * gain_ref[...]).astype(BF16)
    for head in range(TEAM):
        columns = slice(head * HEAD_DIM, (head + 1) * HEAD_DIM)
        slot = head ^ mask_ref[0]
        out_ref[slot, :, :HEAD_DIM] = normed[:, columns]
        out_ref[slot, :, HEAD_DIM:] = value_ref[:, columns]


def query_norm_kernel(mask_ref, span_ref, *refs):
    sources, (out_ref, counts_ref), targets, semaphores = refs[:4], refs[4:6], refs[6:10], refs[10]
    query_ref, grad_ref, gain_ref, docs_ref = fetched(sources, targets, semaphores)
    values = query_ref[...].astype(F32)
    normed = (values * inverse_rms(values) * gain_ref[...]).astype(BF16)
    for head in range(TEAM):
        columns = slice(head * Q_COLS, (head + 1) * Q_COLS)
        slot = head ^ mask_ref[0]
        out_ref[slot, :, :Q_COLS] = normed[:, columns]
        out_ref[slot, :, Q_COLS:] = grad_ref[:, columns]
    lengths = docs_ref[...]
    count = lengths.shape[1]
    earlier = lax.broadcasted_iota(jnp.int32, (count, count), 1) <= lax.broadcasted_iota(
        jnp.int32, (count, count), 0
    )
    ends = jnp.sum(jnp.where(earlier, lengths, 0), axis=1, keepdims=True)
    first = SPAN * (span_ref[0] - 1) + 1
    places = first + lax.broadcasted_iota(jnp.int32, (count, 128), 1)
    found = jnp.sum((ends <= places).astype(jnp.int32), axis=0, keepdims=True)
    found = jnp.where(places[:1] >= 0, found, -1)
    lane = lax.broadcasted_iota(jnp.int32, found.shape, 1)
    for z in range(SPAN):
        mine = found[:, SPAN - 1 + z : SPAN + z]
        near = (lane >= z) & (lane < z + SPAN)
        counts_ref[z] = jnp.sum(((found == mine) & near).astype(jnp.int32))


def contract(left, right, dims):
    return lax.dot_general(left, right, (dims, ((), ())), preferred_element_type=F32)


def attention_kernel(
    slot_ref,
    counts_ref,
    qd_ref,
    own_ref,
    near_ref,
    d_own_ref,
    d_near_ref,
    part_ref,
    dq_0_ref,
    dq_1_ref,
    dq_2_ref,
    dq_3_ref,
    s_ref,
    g_ref,
    p_ref,
    ds_ref,
    dq_ref,
    kv_ref,
    d_kv_ref,
    sums_ref,
):
    border = (SPAN - 1) * BLOCK
    kv_ref[:border] = near_ref[...]
    kv_ref[border:] = own_ref[...]
    d_kv_ref[...] = jnp.zeros_like(d_kv_ref)
    sums_ref[...] = jnp.zeros_like(sums_ref)
    causal = lax.broadcasted_iota(jnp.int32, (BLOCK, BLOCK), 0) <= lax.broadcasted_iota(
        jnp.int32, (BLOCK, BLOCK), 1
    )
    diagonal = jnp.where(causal, 0.0, MASKED)
    factor = SCALE * LOG2E
    half = BLOCK // 2

    def attend(z, count):
        rows = pl.ds(pl.multiple_of(z * BLOCK, BLOCK), BLOCK)
        window = pl.ds(pl.multiple_of((z + SPAN - count) * BLOCK, BLOCK), count * BLOCK)
        spans = [slice(place * BLOCK, (place + 1) * BLOCK) for place in range(count)]
        used = slice(0, count * BLOCK)
        heads = [slice(j * HEAD_DIM, (j + 1) * HEAD_DIM) for j in range(GROUP)]
        queries = jnp.concatenate([qd_ref[rows, lanes] for lanes in heads], axis=0)
        grads = jnp.concatenate(
            [qd_ref[rows, Q_COLS + j * HEAD_DIM : Q_COLS + (j + 1) * HEAD_DIM] for j in range(GROUP)],
            axis=0,
        )
        keys = kv_ref[window, :HEAD_DIM]
        values = kv_ref[window, HEAD_DIM:]
        s_ref[used] = contract(keys, queries, ((1,), (1,)))
        g_ref[used] = contract(values, grads, ((1,), (1,)))
        for lanes in heads:
            tiles = [s_ref[span, lanes] * factor for span in spans]
            tiles[-1] = tiles[-1] + diagonal
            highest = functools.reduce(
                jnp.maximum, [jnp.max(t, axis=0, keepdims=True) for t in tiles]
            )
            tiles = [jnp.exp2(t - highest) for t in tiles]
            total = functools.reduce(jnp.add, [jnp.sum(t, axis=0, keepdims=True) for t in tiles])
            recip = 1.0 / total
            delta = 0.0
            kept = []
            for tile, span in zip(tiles, spans):
                weights = tile * recip
                probs = weights.astype(BF16)
                p_ref[span, lanes] = probs
                kept.append(weights)
                delta = delta + jnp.sum(
                    probs.astype(F32) * g_ref[span, lanes], axis=0, keepdims=True
                )
            for weights, span in zip(kept, spans):
                ds_ref[span, lanes] = (weights * (g_ref[span, lanes] - delta)).astype(BF16)
        score_grads = ds_ref[used]
        d_kv_ref[window, :HEAD_DIM] += contract(score_grads, queries, ((1,), (0,)))
        d_kv_ref[window, HEAD_DIM:] += contract(p_ref[used], grads, ((1,), (0,)))
        d_query = contract(jnp.transpose(keys), score_grads, ((1,), (0,)))
        d_query = (d_query * SCALE).astype(BF16)
        for lanes in heads:
            grad = jnp.transpose(d_query[:, lanes])
            dq_ref[2 * z, :, lanes] = grad[:half]
            dq_ref[2 * z + 1, :, lanes] = grad[half:]
            normed = qd_ref[rows, lanes].astype(F32)
            sums_ref[:1, lanes] += jnp.sum(grad.astype(F32) * normed, axis=0, keepdims=True)

    @pl.loop(0, SPAN)
    def _(z):
        for count in range(1, SPAN + 1):
            pl.when(counts_ref[z] == count)(functools.partial(attend, z, count))

    part_ref[...] = jnp.broadcast_to(sums_ref[:1][None], part_ref.shape)
    for apart, out_ref in enumerate((dq_0_ref, dq_1_ref, dq_2_ref, dq_3_ref)):
        for core in range(2):
            out_ref[core] = dq_ref[2 * ((slot_ref[0] // 2) ^ apart) + core]
    d_near_ref[:, :HEAD_DIM] = (d_kv_ref[:border, :HEAD_DIM] * SCALE).astype(BF16)
    d_near_ref[:, HEAD_DIM:] = d_kv_ref[:border, HEAD_DIM:].astype(BF16)
    d_own_ref[:, :HEAD_DIM] = d_kv_ref[border:, :HEAD_DIM] * SCALE
    d_own_ref[:, HEAD_DIM:] = d_kv_ref[border:, HEAD_DIM:]


def gather_kernel(
    slot_ref, own_ref, near_ref, sums_ref, dq_0_ref, dq_3_ref, dq_2_ref, dq_1_ref, out_ref, keep_ref, give_ref
):
    half = BLOCK // 2
    rest = jnp.sum(sums_ref[...], axis=0)
    pieces = []
    for _ in range(3):
        piece = rest.astype(BF16).astype(F32)
        pieces += [piece[:, at : at + HEAD_DIM] for at in range(0, Q_COLS, HEAD_DIM)]
        rest = rest - piece
    pieces.append(jnp.zeros((SUM_ROWS - len(pieces), HEAD_DIM), F32))
    sums = jnp.concatenate(pieces, axis=0).astype(BF16)
    for slot in range(TEAM):
        rows = slice(slot * half, (slot + 1) * half)
        total = own_ref[rows]
        if slot >= 2:
            total = total + near_ref[(slot - 2) * half : (slot - 1) * half].astype(F32)
        total = total.astype(BF16)
        out_ref[slot, :half] = total[:, :HEAD_DIM]
        out_ref[slot, half:BLOCK] = total[:, HEAD_DIM:]
        out_ref[slot, BLOCK:] = sums
    core = slot_ref[0] % 2
    for apart, dq_ref in enumerate((dq_0_ref, dq_1_ref, dq_2_ref, dq_3_ref)):
        keep_ref[apart] = dq_ref[core]
        give_ref[apart] = dq_ref[1 - core]


def norm_backward(rows, gain, grad):
    values = rows.astype(F32)
    inverse = inverse_rms(values)
    scaled = grad.astype(F32) * gain
    inner = jnp.mean(scaled * values, axis=-1, keepdims=True)
    return (inverse * scaled - values * (inverse * inverse * inverse * inner)).astype(BF16)


def query_back_kernel(head_ref, query_ref, gain_ref, kept_ref, given_ref, out_ref, grad_ref):
    for apart in range(CHIPS):
        for other, source in enumerate((kept_ref, given_ref)):
            head = head_ref[0] ^ (2 * apart + other)
            grad_ref[:, pl.ds(pl.multiple_of(head * Q_COLS, Q_COLS), Q_COLS)] = source[apart]
    out_ref[...] = norm_backward(query_ref[...], gain_ref[...], grad_ref[...])


def key_back_kernel(
    mask_ref,
    key_ref,
    query_gain_ref,
    key_gain_ref,
    back_ref,
    d_key_ref,
    d_value_ref,
    d_query_gain_ref,
    d_key_gain_ref,
):
    half = BLOCK // 2
    slots = [head ^ mask_ref[0] for head in range(TEAM)]
    grad = jnp.concatenate([back_ref[slot, :half] for slot in slots], axis=1)
    d_key_ref[...] = norm_backward(key_ref[...], key_gain_ref[...], grad)
    for head, slot in enumerate(slots):
        columns = slice(head * HEAD_DIM, (head + 1) * HEAD_DIM)
        d_value_ref[:, columns] = back_ref[slot, half:BLOCK]
        pieces = back_ref[slot, BLOCK:].astype(F32)
        sums = pieces[:GROUP] + pieces[GROUP : 2 * GROUP] + pieces[2 * GROUP : 3 * GROUP]
        for j in range(GROUP):
            at = slice((head * GROUP + j) * HEAD_DIM, (head * GROUP + j + 1) * HEAD_DIM)
            d_query_gain_ref[:, at] = sums[j : j + 1] / query_gain_ref[:, at]
        whole = jnp.sum(sums, axis=0, keepdims=True)
        d_key_gain_ref[:, columns] = whole / key_gain_ref[:, columns]


def team_of(seq_at, head_at, seq_count):
    upper = head_at // 4
    segment = seq_at + upper * (2 * seq_count - 1 - 2 * seq_at)
    slot = (segment % 2) * 4 + head_at % 4
    mask = ((seq_at // 2) % 2 ^ upper) * 4 + (seq_at // (seq_count // 2)) * 2
    return segment // 2, slot, mask


def layout(seq_count):
    spans = seq_count
    teams = [[None] * TEAM for _ in range(spans)]
    by_head = [[None] * spans for _ in range(TEAM)]
    for seq_at in range(seq_count):
        for head_at in range(TEAM):
            span, slot, mask = team_of(seq_at, head_at, seq_count)
            device = seq_at * TEAM + head_at
            teams[span][slot] = device
            by_head[slot ^ mask][span] = device
    return teams, by_head


def body(query_raw, key_raw, value_in, out_grad, query_gain, key_gain, doc_blocks):
    seq_count = lax.axis_size("seq")
    axes = ("seq", "head")
    teams, by_head = layout(seq_count)
    span, slot, mask = team_of(lax.axis_index("seq"), lax.axis_index("head"), seq_count)
    mask_scalar = mask[None].astype(jnp.int32)
    slot_scalar = slot[None].astype(jnp.int32)
    head_scalar = (slot ^ mask)[None].astype(jnp.int32)
    span_scalar = span[None].astype(jnp.int32)
    rows = query_raw.shape[1]
    query_rows, key_rows, value_rows, grad_rows = (
        query_raw[0],
        key_raw[0],
        value_in[0],
        out_grad[0],
    )
    query_gain_row, key_gain_row = query_gain[None], key_gain[None]

    def exchange(array):
        return lax.all_to_all(array, axes, 0, 0, axis_index_groups=teams, tiled=True)

    onward = [(line[at], line[at + 1]) for line in by_head for at in range(len(line) - 1)]
    onward.sort()
    backward = sorted((target, source) for source, target in onward)

    kv_send = call(
        key_norm_kernel,
        jax.ShapeDtypeStruct((TEAM, rows, KV_COLS), BF16),
        (mask_scalar, key_rows, value_rows, key_gain_row),
        smem=1,
        far=True,
    )
    own = exchange(kv_send).reshape(TEAM * rows, KV_COLS)
    near = lax.ppermute(own[BLOCK:], axes, onward)
    qd_send, counts = call(
        query_norm_kernel,
        (
            jax.ShapeDtypeStruct((TEAM, rows, 2 * Q_COLS), BF16),
            jax.ShapeDtypeStruct((SPAN,), jnp.int32),
        ),
        (mask_scalar, span_scalar, query_rows, grad_rows, query_gain_row, doc_blocks[None]),
        smem=2,
        smem_out=1,
        far=True,
    )
    qd = exchange(qd_send).reshape(TEAM * rows, 2 * Q_COLS)
    window = SPAN * BLOCK
    d_own, d_near, part, *dq = call(
        attention_kernel,
        (
            jax.ShapeDtypeStruct((window, KV_COLS), F32),
            jax.ShapeDtypeStruct((window - BLOCK, KV_COLS), BF16),
            jax.ShapeDtypeStruct((seq_count, 1, Q_COLS), F32),
        )
        + (jax.ShapeDtypeStruct((2, rows, Q_COLS), BF16),) * CHIPS,
        (slot_scalar, counts, qd, own, near),
        smem=2,
        scratch=[
            pltpu.VMEM((window, Q_COLS), F32),
            pltpu.VMEM((window, Q_COLS), F32),
            pltpu.VMEM((window, Q_COLS), BF16),
            pltpu.VMEM((window, Q_COLS), BF16),
            pltpu.VMEM((TEAM, rows, Q_COLS), BF16),
            pltpu.VMEM((WINDOW * BLOCK, KV_COLS), BF16),
            pltpu.VMEM((WINDOW * BLOCK, KV_COLS), F32),
            pltpu.VMEM((8, Q_COLS), F32),
        ],
    )

    def within(array, apart):
        pairs = [(team[at], team[at ^ apart]) for team in teams for at in range(TEAM)]
        return lax.ppermute(array, axes, sorted(pairs))

    back_near = lax.ppermute(d_near, axes, backward)
    sums = lax.all_to_all(part, axes, 0, 0, axis_index_groups=by_head, tiled=True)
    moved = {apart: within(dq[apart], 2 * apart) for apart in (3, 2, 1)}
    dq = [dq[0]] + [moved[apart] for apart in range(1, CHIPS)]
    back_send, keep, give = call(
        gather_kernel,
        (
            jax.ShapeDtypeStruct((TEAM, 2 * rows + SUM_ROWS, HEAD_DIM), BF16),
            jax.ShapeDtypeStruct((CHIPS, rows, Q_COLS), BF16),
            jax.ShapeDtypeStruct((CHIPS, rows, Q_COLS), BF16),
        ),
        (slot_scalar, d_own, back_near, sums, dq[0], dq[3], dq[2], dq[1]),
        smem=1,
    )
    back = exchange(back_send)
    given = within(give, 1)
    d_query = call(
        query_back_kernel,
        jax.ShapeDtypeStruct(query_rows.shape, BF16),
        (head_scalar, query_rows, query_gain_row, keep, given),
        smem=1,
        scratch=[pltpu.VMEM(query_rows.shape, BF16)],
    )
    d_key, d_value, d_query_gain, d_key_gain = call(
        key_back_kernel,
        (
            jax.ShapeDtypeStruct(key_rows.shape, BF16),
            jax.ShapeDtypeStruct(value_rows.shape, BF16),
            jax.ShapeDtypeStruct(query_gain_row.shape, F32),
            jax.ShapeDtypeStruct(key_gain_row.shape, F32),
        ),
        (mask_scalar, key_rows, query_gain_row, key_gain_row, back),
        smem=1,
    )
    return d_query[None], d_key[None], d_value[None], d_query_gain[0], d_key_gain[0]


def solution(mesh):
    split = P("seq", "head", None)
    in_specs = (split, split, split, split, P(), P(), P())
    out_specs = (split, split, split, P(), P())
    return jax.shard_map(body, mesh=mesh, in_specs=in_specs, out_specs=out_specs, check_vma=False)
```

```python
import functools
import math

import jax
import jax.numpy as jnp
from jax import lax
from jax.experimental import pallas as pl
from jax.experimental.pallas import tpu as pltpu
from jax.sharding import PartitionSpec as P

GROUP = 5
HEAD_DIM = 128
BLOCK = 128
EPSILON = 1e-06
MASKED = -1e30
TEAM = 8
SPAN = 4
WINDOW = 2 * SPAN - 1
Q_COLS = GROUP * HEAD_DIM
KV_COLS = 2 * HEAD_DIM
CHIPS = TEAM // 2
SUM_ROWS = 16
SCALE = 1.0 / math.sqrt(HEAD_DIM)
LOG2E = math.log2(math.e)
F32 = jnp.float32
BF16 = jnp.bfloat16
VMEM_LIMIT = 14 * 1024 * 1024
VMEM_ALL = 63 * 1024 * 1024


def call(kernel, out_shape, args, smem=0, smem_out=0, flops=0, size=1024, scratch=(), far=False):
    whole = pl.BlockSpec(memory_space=pltpu.VMEM)
    scalar = pl.BlockSpec(memory_space=pltpu.SMEM)
    given = pl.BlockSpec(memory_space=pltpu.HBM) if far else whole
    single = not isinstance(out_shape, (tuple, list))
    scratch = list(scratch)
    if far:
        arrays = args[smem:]
        scratch += [pltpu.VMEM(array.shape, array.dtype) for array in arrays]
        scratch += [pltpu.SemaphoreType.DMA((len(arrays),))]
    return pl.pallas_call(
        kernel,
        out_shape=out_shape,
        in_specs=[scalar] * smem + [given] * (len(args) - smem),
        out_specs=whole
        if single
        else [whole] * (len(out_shape) - smem_out) + [scalar] * smem_out,
        scratch_shapes=scratch,
        compiler_params=pltpu.CompilerParams(vmem_limit_bytes=VMEM_ALL if far else VMEM_LIMIT),
        cost_estimate=pl.CostEstimate(flops=flops, bytes_accessed=size, transcendentals=0),
    )(*args)


def fetched(sources, targets, semaphores):
    copies = [
        pltpu.make_async_copy(source, target, semaphores.at[at])
        for at, (source, target) in enumerate(zip(sources, targets))
    ]
    for copy in copies:
        copy.start()
    for copy in copies:
        copy.wait()
    return targets


def inverse_rms(values):
    return lax.rsqrt(jnp.mean(values * values, axis=-1, keepdims=True) + EPSILON)


def key_norm_kernel(
    mask_ref, key_in, value_in, gain_in, out_ref, key_ref, value_ref, gain_ref, semaphores
):
    fetched((key_in, value_in, gain_in), (key_ref, value_ref, gain_ref), semaphores)
    values = key_ref[...].astype(F32)
    normed = (values * inverse_rms(values) * gain_ref[...]).astype(BF16)
    for head in range(TEAM):
        columns = slice(head * HEAD_DIM, (head + 1) * HEAD_DIM)
        slot = head ^ mask_ref[0]
        out_ref[slot, :, :HEAD_DIM] = normed[:, columns]
        out_ref[slot, :, HEAD_DIM:] = value_ref[:, columns]


def query_norm_kernel(mask_ref, span_ref, *refs):
    sources, (out_ref, inverse_ref, counts_ref) = refs[:4], refs[4:7]
    targets, semaphores = refs[7:11], refs[11]
    query_ref, grad_ref, gain_ref, docs_ref = fetched(sources, targets, semaphores)
    values = query_ref[...].astype(F32)
    inverse = inverse_rms(values)
    inverse_ref[...] = jnp.broadcast_to(inverse, inverse_ref.shape)
    normed = (values * inverse * gain_ref[...]).astype(BF16)
    for head in range(TEAM):
        columns = slice(head * Q_COLS, (head + 1) * Q_COLS)
        slot = head ^ mask_ref[0]
        out_ref[slot, :, :Q_COLS] = normed[:, columns]
        out_ref[slot, :, Q_COLS:] = grad_ref[:, columns]
    lengths = docs_ref[...]
    count = lengths.shape[1]
    earlier = lax.broadcasted_iota(jnp.int32, (count, count), 1) <= lax.broadcasted_iota(
        jnp.int32, (count, count), 0
    )
    ends = jnp.sum(jnp.where(earlier, lengths, 0), axis=1, keepdims=True)
    first = SPAN * (span_ref[0] - 1) + 1
    places = first + lax.broadcasted_iota(jnp.int32, (count, 128), 1)
    found = jnp.sum((ends <= places).astype(jnp.int32), axis=0, keepdims=True)
    found = jnp.where(places[:1] >= 0, found, -1)
    lane = lax.broadcasted_iota(jnp.int32, found.shape, 1)
    for z in range(SPAN):
        mine = found[:, SPAN - 1 + z : SPAN + z]
        near = (lane >= z) & (lane < z + SPAN)
        counts_ref[z] = jnp.sum(((found == mine) & near).astype(jnp.int32))


def contract(left, right, dims):
    return lax.dot_general(left, right, (dims, ((), ())), preferred_element_type=F32)


def attention_kernel(
    slot_ref,
    counts_ref,
    qd_ref,
    own_ref,
    near_ref,
    d_own_ref,
    d_near_ref,
    part_ref,
    dq_0_ref,
    dq_1_ref,
    dq_2_ref,
    dq_3_ref,
    s_ref,
    g_ref,
    p_ref,
    ds_ref,
    dq_ref,
    kv_ref,
    d_kv_ref,
    sums_ref,
):
    border = (SPAN - 1) * BLOCK
    kv_ref[:border] = near_ref[...]
    kv_ref[border:] = own_ref[...]
    d_kv_ref[...] = jnp.zeros_like(d_kv_ref)
    sums_ref[...] = jnp.zeros_like(sums_ref)
    causal = lax.broadcasted_iota(jnp.int32, (BLOCK, BLOCK), 0) <= lax.broadcasted_iota(
        jnp.int32, (BLOCK, BLOCK), 1
    )
    diagonal = jnp.where(causal, 0.0, MASKED)
    factor = SCALE * LOG2E
    half = BLOCK // 2

    def attend(z, count):
        rows = pl.ds(pl.multiple_of(z * BLOCK, BLOCK), BLOCK)
        window = pl.ds(pl.multiple_of((z + SPAN - count) * BLOCK, BLOCK), count * BLOCK)
        spans = [slice(place * BLOCK, (place + 1) * BLOCK) for place in range(count)]
        used = slice(0, count * BLOCK)
        heads = [slice(j * HEAD_DIM, (j + 1) * HEAD_DIM) for j in range(GROUP)]
        queries = jnp.concatenate([qd_ref[rows, lanes] for lanes in heads], axis=0)
        grads = jnp.concatenate(
            [qd_ref[rows, Q_COLS + j * HEAD_DIM : Q_COLS + (j + 1) * HEAD_DIM] for j in range(GROUP)],
            axis=0,
        )
        keys = kv_ref[window, :HEAD_DIM]
        values = kv_ref[window, HEAD_DIM:]
        s_ref[used] = contract(keys, queries, ((1,), (1,)))
        g_ref[used] = contract(values, grads, ((1,), (1,)))
        for lanes in heads:
            tiles = [s_ref[span, lanes] * factor for span in spans]
            tiles[-1] = tiles[-1] + diagonal
            highest = functools.reduce(
                jnp.maximum, [jnp.max(t, axis=0, keepdims=True) for t in tiles]
            )
            tiles = [jnp.exp2(t - highest) for t in tiles]
            total = functools.reduce(jnp.add, [jnp.sum(t, axis=0, keepdims=True) for t in tiles])
            recip = 1.0 / total
            delta = 0.0
            kept = []
            for tile, span in zip(tiles, spans):
                weights = tile * recip
                probs = weights.astype(BF16)
                p_ref[span, lanes] = probs
                kept.append(weights)
                delta = delta + jnp.sum(
                    probs.astype(F32) * g_ref[span, lanes], axis=0, keepdims=True
                )
            for weights, span in zip(kept, spans):
                ds_ref[span, lanes] = (weights * (g_ref[span, lanes] - delta)).astype(BF16)
        score_grads = ds_ref[used]
        d_kv_ref[window, :HEAD_DIM] += contract(score_grads, queries, ((1,), (0,)))
        d_kv_ref[window, HEAD_DIM:] += contract(p_ref[used], grads, ((1,), (0,)))
        d_query = contract(jnp.transpose(keys), score_grads, ((1,), (0,)))
        d_query = (d_query * SCALE).astype(BF16)
        for lanes in heads:
            grad = jnp.transpose(d_query[:, lanes])
            dq_ref[2 * z, :, lanes] = grad[:half]
            dq_ref[2 * z + 1, :, lanes] = grad[half:]
            normed = qd_ref[rows, lanes].astype(F32)
            sums_ref[:1, lanes] += jnp.sum(grad.astype(F32) * normed, axis=0, keepdims=True)

    @pl.loop(0, SPAN)
    def _(z):
        for count in range(1, SPAN + 1):
            pl.when(counts_ref[z] == count)(functools.partial(attend, z, count))

    part_ref[...] = jnp.broadcast_to(sums_ref[:1][None], part_ref.shape)
    for apart, out_ref in enumerate((dq_0_ref, dq_1_ref, dq_2_ref, dq_3_ref)):
        for core in range(2):
            out_ref[core] = dq_ref[2 * ((slot_ref[0] // 2) ^ apart) + core]
    d_near_ref[:, :HEAD_DIM] = (d_kv_ref[:border, :HEAD_DIM] * SCALE).astype(BF16)
    d_near_ref[:, HEAD_DIM:] = d_kv_ref[:border, HEAD_DIM:].astype(BF16)
    d_own_ref[:, :HEAD_DIM] = d_kv_ref[border:, :HEAD_DIM] * SCALE
    d_own_ref[:, HEAD_DIM:] = d_kv_ref[border:, HEAD_DIM:]


def gather_kernel(
    slot_ref, own_ref, near_ref, sums_ref, dq_0_ref, dq_3_ref, dq_2_ref, dq_1_ref, out_ref, keep_ref, give_ref
):
    half = BLOCK // 2
    rest = jnp.sum(sums_ref[...], axis=0)
    pieces = []
    for _ in range(3):
        piece = rest.astype(BF16).astype(F32)
        pieces += [piece[:, at : at + HEAD_DIM] for at in range(0, Q_COLS, HEAD_DIM)]
        rest = rest - piece
    pieces.append(jnp.zeros((SUM_ROWS - len(pieces), HEAD_DIM), F32))
    sums = jnp.concatenate(pieces, axis=0).astype(BF16)
    for slot in range(TEAM):
        rows = slice(slot * half, (slot + 1) * half)
        total = own_ref[rows]
        if slot >= 2:
            total = total + near_ref[(slot - 2) * half : (slot - 1) * half].astype(F32)
        total = total.astype(BF16)
        out_ref[slot, :half] = total[:, :HEAD_DIM]
        out_ref[slot, half:BLOCK] = total[:, HEAD_DIM:]
        out_ref[slot, BLOCK:] = sums
    core = slot_ref[0] % 2
    for apart, dq_ref in enumerate((dq_0_ref, dq_1_ref, dq_2_ref, dq_3_ref)):
        keep_ref[apart] = dq_ref[core]
        give_ref[apart] = dq_ref[1 - core]


def norm_backward(rows, gain, grad, inverse=None):
    values = rows.astype(F32)
    inverse = inverse_rms(values) if inverse is None else inverse
    scaled = grad.astype(F32) * gain
    inner = jnp.mean(scaled * values, axis=-1, keepdims=True)
    return (inverse * scaled - values * (inverse * inverse * inverse * inner)).astype(BF16)


def query_back_kernel(
    head_ref, query_ref, gain_ref, inverse_ref, kept_ref, given_ref, out_ref, grad_ref
):
    for apart in range(CHIPS):
        for other, source in enumerate((kept_ref, given_ref)):
            head = head_ref[0] ^ (2 * apart + other)
            grad_ref[:, pl.ds(pl.multiple_of(head * Q_COLS, Q_COLS), Q_COLS)] = source[apart]
    out_ref[...] = norm_backward(
        query_ref[...], gain_ref[...], grad_ref[...], inverse_ref[:, :1]
    )


def key_back_kernel(
    mask_ref,
    key_ref,
    query_gain_ref,
    key_gain_ref,
    back_ref,
    d_key_ref,
    d_value_ref,
    d_query_gain_ref,
    d_key_gain_ref,
):
    half = BLOCK // 2
    slots = [head ^ mask_ref[0] for head in range(TEAM)]
    grad = jnp.concatenate([back_ref[slot, :half] for slot in slots], axis=1)
    d_key_ref[...] = norm_backward(key_ref[...], key_gain_ref[...], grad)
    for head, slot in enumerate(slots):
        columns = slice(head * HEAD_DIM, (head + 1) * HEAD_DIM)
        d_value_ref[:, columns] = back_ref[slot, half:BLOCK]
        pieces = back_ref[slot, BLOCK:].astype(F32)
        sums = pieces[:GROUP] + pieces[GROUP : 2 * GROUP] + pieces[2 * GROUP : 3 * GROUP]
        for j in range(GROUP):
            at = slice((head * GROUP + j) * HEAD_DIM, (head * GROUP + j + 1) * HEAD_DIM)
            d_query_gain_ref[:, at] = sums[j : j + 1] / query_gain_ref[:, at]
        whole = jnp.sum(sums, axis=0, keepdims=True)
        d_key_gain_ref[:, columns] = whole / key_gain_ref[:, columns]


def team_of(seq_at, head_at, seq_count):
    upper = head_at // 4
    segment = seq_at + upper * (2 * seq_count - 1 - 2 * seq_at)
    slot = (segment % 2) * 4 + head_at % 4
    mask = ((seq_at // 2) % 2 ^ upper) * 4 + (seq_at // (seq_count // 2)) * 2
    return segment // 2, slot, mask


def layout(seq_count):
    spans = seq_count
    teams = [[None] * TEAM for _ in range(spans)]
    by_head = [[None] * spans for _ in range(TEAM)]
    for seq_at in range(seq_count):
        for head_at in range(TEAM):
            span, slot, mask = team_of(seq_at, head_at, seq_count)
            device = seq_at * TEAM + head_at
            teams[span][slot] = device
            by_head[slot ^ mask][span] = device
    return teams, by_head


def body(query_raw, key_raw, value_in, out_grad, query_gain, key_gain, doc_blocks):
    seq_count = lax.axis_size("seq")
    axes = ("seq", "head")
    teams, by_head = layout(seq_count)
    span, slot, mask = team_of(lax.axis_index("seq"), lax.axis_index("head"), seq_count)
    mask_scalar = mask[None].astype(jnp.int32)
    slot_scalar = slot[None].astype(jnp.int32)
    head_scalar = (slot ^ mask)[None].astype(jnp.int32)
    span_scalar = span[None].astype(jnp.int32)
    rows = query_raw.shape[1]
    query_rows, key_rows, value_rows, grad_rows = (
        query_raw[0],
        key_raw[0],
        value_in[0],
        out_grad[0],
    )
    query_gain_row, key_gain_row = query_gain[None], key_gain[None]

    def exchange(array):
        return lax.all_to_all(array, axes, 0, 0, axis_index_groups=teams, tiled=True)

    onward = [(line[at], line[at + 1]) for line in by_head for at in range(len(line) - 1)]
    onward.sort()
    backward = sorted((target, source) for source, target in onward)

    kv_send = call(
        key_norm_kernel,
        jax.ShapeDtypeStruct((TEAM, rows, KV_COLS), BF16),
        (mask_scalar, key_rows, value_rows, key_gain_row),
        smem=1,
        far=True,
    )
    own = exchange(kv_send).reshape(TEAM * rows, KV_COLS)
    near = lax.ppermute(own[BLOCK:], axes, onward)
    qd_send, inverse, counts = call(
        query_norm_kernel,
        (
            jax.ShapeDtypeStruct((TEAM, rows, 2 * Q_COLS), BF16),
            jax.ShapeDtypeStruct((rows, 128), F32),
            jax.ShapeDtypeStruct((SPAN,), jnp.int32),
        ),
        (mask_scalar, span_scalar, query_rows, grad_rows, query_gain_row, doc_blocks[None]),
        smem=2,
        smem_out=1,
        far=True,
    )
    qd = exchange(qd_send).reshape(TEAM * rows, 2 * Q_COLS)
    window = SPAN * BLOCK
    d_own, d_near, part, *dq = call(
        attention_kernel,
        (
            jax.ShapeDtypeStruct((window, KV_COLS), F32),
            jax.ShapeDtypeStruct((window - BLOCK, KV_COLS), BF16),
            jax.ShapeDtypeStruct((seq_count, 1, Q_COLS), F32),
        )
        + (jax.ShapeDtypeStruct((2, rows, Q_COLS), BF16),) * CHIPS,
        (slot_scalar, counts, qd, own, near),
        smem=2,
        scratch=[
            pltpu.VMEM((window, Q_COLS), F32),
            pltpu.VMEM((window, Q_COLS), F32),
            pltpu.VMEM((window, Q_COLS), BF16),
            pltpu.VMEM((window, Q_COLS), BF16),
            pltpu.VMEM((TEAM, rows, Q_COLS), BF16),
            pltpu.VMEM((WINDOW * BLOCK, KV_COLS), BF16),
            pltpu.VMEM((WINDOW * BLOCK, KV_COLS), F32),
            pltpu.VMEM((8, Q_COLS), F32),
        ],
    )

    def within(array, apart):
        pairs = [(team[at], team[at ^ apart]) for team in teams for at in range(TEAM)]
        return lax.ppermute(array, axes, sorted(pairs))

    back_near = lax.ppermute(d_near, axes, backward)
    sums = lax.all_to_all(part, axes, 0, 0, axis_index_groups=by_head, tiled=True)
    moved = {apart: within(dq[apart], 2 * apart) for apart in (3, 2, 1)}
    dq = [dq[0]] + [moved[apart] for apart in range(1, CHIPS)]
    back_send, keep, give = call(
        gather_kernel,
        (
            jax.ShapeDtypeStruct((TEAM, 2 * rows + SUM_ROWS, HEAD_DIM), BF16),
            jax.ShapeDtypeStruct((CHIPS, rows, Q_COLS), BF16),
            jax.ShapeDtypeStruct((CHIPS, rows, Q_COLS), BF16),
        ),
        (slot_scalar, d_own, back_near, sums, dq[0], dq[3], dq[2], dq[1]),
        smem=1,
    )
    back = exchange(back_send)
    given = within(give, 1)
    d_query = call(
        query_back_kernel,
        jax.ShapeDtypeStruct(query_rows.shape, BF16),
        (head_scalar, query_rows, query_gain_row, inverse, keep, given),
        smem=1,
        scratch=[pltpu.VMEM(query_rows.shape, BF16)],
    )
    d_key, d_value, d_query_gain, d_key_gain = call(
        key_back_kernel,
        (
            jax.ShapeDtypeStruct(key_rows.shape, BF16),
            jax.ShapeDtypeStruct(value_rows.shape, BF16),
            jax.ShapeDtypeStruct(query_gain_row.shape, F32),
            jax.ShapeDtypeStruct(key_gain_row.shape, F32),
        ),
        (mask_scalar, key_rows, query_gain_row, key_gain_row, back),
        smem=1,
    )
    return d_query[None], d_key[None], d_value[None], d_query_gain[0], d_key_gain[0]


def solution(mesh):
    split = P("seq", "head", None)
    in_specs = (split, split, split, split, P(), P(), P())
    out_specs = (split, split, split, P(), P())
    return jax.shard_map(body, mesh=mesh, in_specs=in_specs, out_specs=out_specs, check_vma=False)
```
